256 devices in a mesh: gx: 8 (over z_lo, core), gy: 32 (over y, x, z_hi).
Axes of the slice: x: 4, y: 4, z: 8 (z_hi: 2, z_lo: 4; z = z_hi * 4 + z_lo), core: 2. Of those that a mesh axis runs over, the one named last changes fastest.
Arguments:
- tokens: bfloat16 [2048, 6144], P('gx', 'gy'), may hold values from -6 to 6
- weight_in: bfloat16 [6144, 16384], P('gx', 'gy'), may hold values from -0.15625 to 0.15625
- weight_out: bfloat16 [16384, 6144], P('gy', 'gx'), may hold values from -0.046875 to 0.046875
- grad_out: bfloat16 [2048, 6144], P('gx', 'gy'), may hold values from -3 to 3
Outputs:
- grad_input: bfloat16 [2048, 6144], P('gx', 'gy')
- grad_weight_in: bfloat16 [6144, 16384], P('gx', 'gy')
- grad_weight_out: bfloat16 [16384, 6144], P('gy', 'gx')
The draws below stay inside these ranges and needn't reach their ends.
All inputs are finite; a program needn't handle non-finite values.
Results may differ from the reference program's by a relative error of at most 0.02.
Values may be sent and summed in bfloat16 or wider, within the bound.
No kernel may reach another device: no remote copies, remote signals or barrier semaphores. Data moves between devices by JAX's collectives and lax.ppermute only.
A program may use at most 128 MiB of HBM per device.

```python
import jax
import jax.numpy as jnp
from jax import lax

D = 6144
FF = 16384
TOK_DEV = 256
TOKENS = 2048


def strengthened(drawn, own_key, source, target, blocks, factor):
    owner, partner = [(jnp.arange(drawn.shape[position]) // (drawn.shape[position] // blocks)).reshape([-1 if axis == position else 1 for axis in range(drawn.ndim)]) for position in (source, target)]
    chosen = jax.random.permutation(own_key, blocks)[partner]
    strong = (owner == chosen) | (owner == (partner + blocks // 2) % blocks)
    return jnp.where(strong, factor * drawn, drawn)


def levels(own_key, dims, pieces, least, top_value):
    loudness = 1.0
    for position, shards_of in pieces:
        heights = jax.random.uniform(jax.random.fold_in(jax.random.fold_in(own_key, 6), position), (shards_of,), jnp.float32, least / len(pieces), top_value / len(pieces))
        loudness = loudness * jnp.repeat(jnp.exp(heights), dims[position] // shards_of).reshape((-1,) + (1,) * (len(dims) - 1 - position))
    return loudness


def noise(key, dims, deviation, limit, cuts=(), kind=jnp.bfloat16):
    values = deviation * jax.random.normal(key, dims, jnp.float32)
    if cuts:
        values = values * levels(key, dims, cuts, -0.22, 0.18)
    return jnp.clip(values, -limit, limit).astype(kind)


def bell_draw_with(rng, extent, scale, reach, shards, heavy, held_as=jnp.bfloat16):
    result = scale * jax.random.normal(rng, extent, jnp.float32)
    if shards:
        result = result * levels(rng, extent, shards, -0.22, 0.18)
    return jnp.clip(strengthened(result, jax.random.fold_in(rng, 3), *heavy), -reach, reach).astype(held_as)


def setup_inputs(seed: int = 0) -> dict:
    key_list = jax.random.split(jax.random.key(seed), 5)
    tokens = bell_draw_with(key_list[0], (TOKENS, D), 1.0, 6.0, ((0, 8), (1, 32)), (0, 1, 32, 2.75))
    weight_in = bell_draw_with(key_list[1], (D, FF), D ** -0.5, 0.15625, ((0, 8), (1, 32)), (1, 0, 32, 2.75))
    weight_out = noise(key_list[2], (FF, D), FF ** -0.5, 0.046875, ((0, 32), (1, 8)))
    grad_out = bell_draw_with(key_list[3], (TOKENS, D), 0.5, 3.0, ((0, 8), (1, 32)), (0, 1, 32, 2.75))
    return {"tokens": tokens, "weight_in": weight_in, "weight_out": weight_out, "grad_out": grad_out}


def gelu_parts(preact):
    normal_cdf = 0.5 * (1.0 + jax.scipy.special.erf(preact * 0.7071067811865476))
    density = jnp.exp(-0.5 * preact * preact) * 0.3989422804014327
    return preact * normal_cdf, normal_cdf + preact * density


def blocked_product(left_rows, right_rows, block_rows):
    blocks = left_rows.shape[0] // block_rows
    start_sum = jnp.zeros((left_rows.shape[1], right_rows.shape[1]), jnp.float32)

    def accumulate(running, block_index):
        left_block = lax.dynamic_slice_in_dim(left_rows, block_index * block_rows, block_rows, 0)
        right_block = lax.dynamic_slice_in_dim(right_rows, block_index * block_rows, block_rows, 0)
        partial_value = lax.dot_general(left_block, right_block, (((0,), (0,)), ((), ())), preferred_element_type=jnp.float32)
        rounded = lax.optimization_barrier(partial_value.astype(jnp.bfloat16))
        return running + rounded.astype(jnp.float32), None

    running, unused = lax.scan(accumulate, start_sum, jnp.arange(blocks, dtype=jnp.int32))
    return running.astype(jnp.bfloat16)


def reference(tokens, weight_in, weight_out, grad_out):
    preact = jnp.dot(tokens, weight_in, preferred_element_type=jnp.float32)
    activated, slope = gelu_parts(preact)
    hidden = activated.astype(jnp.bfloat16)
    grad_hidden = lax.dot_general(grad_out, weight_out, (((1,), (1,)), ((), ())), preferred_element_type=jnp.float32)
    grad_pre = (grad_hidden * slope).astype(jnp.bfloat16)
    grad_input = lax.dot_general(grad_pre, weight_in, (((1,), (1,)), ((), ())), preferred_element_type=jnp.float32).astype(jnp.bfloat16)
    grad_weight_in = blocked_product(tokens, grad_pre, TOK_DEV)
    grad_weight_out = blocked_product(hidden, grad_out, TOK_DEV)
    return grad_input, grad_weight_in, grad_weight_out
```

```python
import functools

import jax
import jax.numpy as jnp
from jax import lax
from jax.experimental import pallas as pl
from jax.experimental.pallas import tpu as pltpu
from jax.sharding import Mesh, PartitionSpec as P

NAMES = ("zl1", "zl0", "c", "y1", "y0", "x1", "x0", "zh")
GX = ("zl1", "zl0", "c")
GY = ("y1", "y0", "x1", "x0", "zh")
YAX = ("y1", "y0")
XAX = ("x1", "x0")
PAIR = ("zl0", "c")
BF = jnp.bfloat16
F32 = jnp.float32


def flip(value, axes, mask):
    size = 1 << len(axes)
    return lax.ppermute(value, axes, [(i, i ^ mask) for i in range(size)])


def transposed(value, flip_zh):
    pairs = []
    for a in range(2):
        for b in range(2):
            for h in range(2):
                pairs.append(((a * 2 + b) * 2 + h, (b * 2 + a) * 2 + (h ^ flip_zh)))
    return lax.ppermute(value, ("zl1", "y1", "zh"), pairs)


def gelu_parts(preact):
    normal_cdf = 0.5 * (1.0 + jax.scipy.special.erf(preact * 0.7071067811865476))
    density = jnp.exp(-0.5 * preact * preact) * 0.3989422804014327
    return preact * normal_cdf, normal_cdf + preact * density


def call(kernel, outs, *operands, flops):
    idx, *arrays = operands
    vmem = pl.BlockSpec(memory_space=pltpu.VMEM)
    size = sum(a.size * a.dtype.itemsize for a in list(arrays) + list(outs))
    return pl.pallas_call(
        kernel,
        out_shape=outs,
        in_specs=[pl.BlockSpec(memory_space=pltpu.SMEM)] + [vmem] * len(arrays),
        out_specs=[vmem] * len(outs),
        compiler_params=pltpu.CompilerParams(vmem_limit_bytes=32 * 1024 * 1024),
        cost_estimate=pl.CostEstimate(flops=flops, bytes_accessed=size, transcendentals=0),
    )(idx, *arrays)


def tile_rows(idx, p, q, r0, s1):
    x0 = idx[3]
    rows = []
    for r1 in range(2):
        r = r1 * 2 + r0
        for half in range(2):
            pair = []
            for s0 in range(2):
                s = s1 * 2 + s0
                pair.append(p[r][s] if half == 0 else q[s][r])
            first = jnp.where(x0 == 0, pair[0], pair[1])
            second = jnp.where(x0 == 0, pair[1], pair[0])
            rows.append(jnp.concatenate([first, second], axis=1))
    return jnp.concatenate(rows, axis=0)


def block_of(idx, r0, s1):
    return (idx[1] ^ r0) * 2 + (idx[2] ^ s1)


def forward_kernel(transposed_weight, idx, w, *refs):
    p, q, (keep, send) = refs[0:4], refs[4:8], refs[8:10]
    total = None
    for r0 in range(2):
        for s1 in range(2):
            rows = tile_rows(idx, p, q, r0, s1)
            weight = w[block_of(idx, r0, s1)]
            term = lax.dot_general(
                rows, weight, (((1,), (1 if transposed_weight else 0,)), ((), ())),
                preferred_element_type=F32,
            )
            total = term if total is None else total + term
    half = total.shape[0] // 2
    low, high = total[:half], total[half:]
    zl1 = idx[0]
    keep[...] = jnp.where(zl1 == 0, low, high)
    send[...] = jnp.where(zl1 == 0, high, low).astype(BF)


def ordered_rows(idx, own, other):
    mine, theirs = own[...], other[...]
    zl1 = idx[0]
    return jnp.concatenate(
        [jnp.where(zl1 == 0, mine, theirs), jnp.where(zl1 == 0, theirs, mine)], axis=0
    )


def weight_grad_kernel(features_first, idx, own, other, *refs):
    p, q, out = refs[0:4], refs[4:8], refs[8]
    hidden = ordered_rows(idx, own, other)
    for r0 in range(2):
        for s1 in range(2):
            rows = tile_rows(idx, p, q, r0, s1)
            left, right = (rows, hidden) if features_first else (hidden, rows)
            term = lax.dot_general(
                left, right, (((0,), (0,)), ((), ())), preferred_element_type=F32
            )
            out[block_of(idx, r0, s1)] = term.astype(BF)


def input_grad_kernel(idx, own, other, w, *refs):
    p, q = refs[0:4], refs[4:8]
    x0 = idx[3]
    grad = ordered_rows(idx, own, other)
    n = p[0].shape[1]
    k2 = p[0].shape[2]
    for r0 in range(2):
        for s1 in range(2):
            term = lax.dot_general(
                grad, w[block_of(idx, r0, s1)], (((1,), (1,)), ((), ())),
                preferred_element_type=F32,
            ).astype(BF)
            first, second = term[:, :k2], term[:, k2:]
            by_s0 = (jnp.where(x0 == 0, first, second), jnp.where(x0 == 0, second, first))
            for s0 in range(2):
                s = s1 * 2 + s0
                for r1 in range(2):
                    r = r1 * 2 + r0
                    base = r1 * 2 * n
                    p[r][s] = by_s0[s0][base:base + n]
                    q[s][r] = by_s0[s0][base + n:base + 2 * n]


def spread(value, axes):
    return [value] + [flip(value, axes, m) for m in (1, 3, 2)]


def in_order(parts):
    zero, one, three, two = parts
    return [zero, one, two, three]


def body(tokens, weight_in, weight_out, grad_out):
    t, k = tokens.shape
    n = t // 2
    f = weight_in.shape[1]
    zl1 = lax.axis_index("zl1")
    zh = lax.axis_index("zh")
    idx = jnp.stack(
        [zl1, lax.axis_index("y0"), lax.axis_index("x1"), lax.axis_index("x0")]
    ).astype(jnp.int32)

    w1 = lax.all_gather(weight_in, PAIR, axis=0)
    w2 = lax.all_gather(weight_out, PAIR, axis=0)

    both = jnp.stack([tokens, grad_out])
    same = transposed(both, 0)
    away = transposed(both, 1)
    tile = jnp.concatenate(
        [jnp.where(zh == 0, same, away), jnp.where(zh == 0, away, same)], axis=2
    )
    first_p = in_order(spread(tile[:, :n], XAX))
    first_q = in_order(spread(tile[:, n:], YAX))

    def second(a):
        p_block = jnp.stack([v[a] for v in first_p])
        q_block = jnp.stack([v[a] for v in first_q])
        return in_order(spread(p_block, YAX)) + in_order(spread(q_block, XAX))

    x_tiles = second(0)
    g_tiles = second(1)

    product = 2 * 2 * t * 4 * w1.shape[1] * f
    halves = [jax.ShapeDtypeStruct((t, f), F32), jax.ShapeDtypeStruct((t, f), BF)]
    pre_keep, pre_send = call(
        functools.partial(forward_kernel, False), halves, idx, w1, *x_tiles, flops=product
    )
    preact = pre_keep + flip(pre_send, ("zl1",), 1).astype(F32)
    activated, slope = gelu_parts(preact)
    hidden = activated.astype(BF)
    hidden_other = flip(hidden, ("zl1",), 1)

    gh_keep, gh_send = call(
        functools.partial(forward_kernel, True), halves, idx, w2, *g_tiles, flops=product
    )
    grad_hidden = gh_keep + flip(gh_send, ("zl1",), 1).astype(F32)
    grad_pre = (grad_hidden * slope).astype(BF)
    grad_pre_other = flip(grad_pre, ("zl1",), 1)

    (terms_out,) = call(
        functools.partial(weight_grad_kernel, False),
        [jax.ShapeDtypeStruct(w2.shape, BF)],
        idx, hidden, hidden_other, *g_tiles, flops=product,
    )
    grad_weight_out = lax.psum_scatter(terms_out, PAIR, scatter_dimension=0)

    piece = jax.ShapeDtypeStruct((4, n, 2 * k), BF)
    pieces = call(
        input_grad_kernel, [piece] * 8, idx, grad_pre, grad_pre_other, w1, flops=product
    )
    p, q = pieces[:4], pieces[4:]

    (terms_in,) = call(
        functools.partial(weight_grad_kernel, True),
        [jax.ShapeDtypeStruct(w1.shape, BF)],
        idx, grad_pre, grad_pre_other, *x_tiles, flops=product,
    )
    grad_weight_in = lax.psum_scatter(terms_in, PAIR, scatter_dimension=0)

    def summed(own, arrived):
        total = own.astype(F32)
        for v in arrived:
            total = total + v.astype(F32)
        return total.astype(BF)

    p_sum = summed(p[0], [flip(p[m], YAX, m) for m in (1, 3, 2)])
    q_sum = summed(q[0], [flip(q[m], XAX, m) for m in (1, 3, 2)])
    p_tile = summed(p_sum[0], [flip(p_sum[m], XAX, m) for m in (1, 3, 2)])
    q_tile = summed(q_sum[0], [flip(q_sum[m], YAX, m) for m in (1, 3, 2)])
    total = jnp.concatenate([p_tile, q_tile], axis=0)
    left, right = total[:, :k], total[:, k:]
    same = transposed(jnp.where(zh == 0, left, right), 0)
    away = transposed(jnp.where(zh == 0, right, left), 1)
    grad_input = (same.astype(F32) + away.astype(F32)).astype(BF)
    return grad_input, grad_weight_in, grad_weight_out


def solution(mesh):
    fine = Mesh(mesh.devices.reshape((2,) * 8), NAMES)
    in_specs = (P(GX, GY), P(GX, GY), P(GY, GX), P(GX, GY))
    out_specs = (P(GX, GY), P(GX, GY), P(GY, GX))
    return jax.shard_map(body, mesh=fine, in_specs=in_specs, out_specs=out_specs, check_vma=False)
```

```python
import functools

import jax
import jax.numpy as jnp
from jax import lax
from jax.experimental import pallas as pl
from jax.experimental.pallas import tpu as pltpu
from jax.sharding import Mesh, PartitionSpec as P

NAMES = ("zl1", "zl0", "c", "y1", "y0", "x1", "x0", "zh")
GX = ("zl1", "zl0", "c")
GY = ("y1", "y0", "x1", "x0", "zh")
YAX = ("y1", "y0")
XAX = ("x1", "x0")
PAIR = ("zl0", "c")
BF = jnp.bfloat16
F32 = jnp.float32


def flip(value, axes, mask):
    size = 1 << len(axes)
    return lax.ppermute(value, axes, [(i, i ^ mask) for i in range(size)])


def transposed(value, flip_zh):
    pairs = []
    for a in range(2):
        for b in range(2):
            for h in range(2):
                pairs.append(((a * 2 + b) * 2 + h, (b * 2 + a) * 2 + (h ^ flip_zh)))
    return lax.ppermute(value, ("zl1", "y1", "zh"), pairs)


def together(*values):
    return lax.optimization_barrier(values)


def gelu_parts(preact):
    normal_cdf = 0.5 * (1.0 + jax.scipy.special.erf(preact * 0.7071067811865476))
    density = jnp.exp(-0.5 * preact * preact) * 0.3989422804014327
    return preact * normal_cdf, normal_cdf + preact * density


def call(kernel, outs, *operands, flops):
    idx, *arrays = operands
    vmem = pl.BlockSpec(memory_space=pltpu.VMEM)
    size = sum(a.size * a.dtype.itemsize for a in list(arrays) + list(outs))
    return pl.pallas_call(
        kernel,
        out_shape=outs,
        in_specs=[pl.BlockSpec(memory_space=pltpu.SMEM)] + [vmem] * len(arrays),
        out_specs=[vmem] * len(outs),
        compiler_params=pltpu.CompilerParams(vmem_limit_bytes=24 * 1024 * 1024),
        cost_estimate=pl.CostEstimate(flops=flops, bytes_accessed=size, transcendentals=0),
    )(idx, *arrays)


PIECES = 10


def look(refs, base, far, place):
    return [
        (0, 0), (1, 0), (3 + place // 2, -2 * (place // 2)), (2, 0),
    ][far] if base == 0 else [
        (0, 0), (1, 2), (3 + place // 2, -2 * (place // 2)), (2, 2),
    ][far]


def p_tile(refs, base, r, s1, s0):
    ref, shift = look(refs, base, r, s1 * 2)
    return refs[ref][s1 * 2 + shift + s0]


def q_tile(refs, base, r, s):
    ref, shift = look(refs, base, s, r)
    return refs[5 + ref][r + shift]


def columns(idx, refs, base, r0, s1):
    x0 = idx[3]
    blocks = []
    for r1 in range(2):
        r = r1 * 2 + r0
        parts = []
        q_own, q_next = (q_tile(refs, base, r, s1 * 2 + s0) for s0 in range(2))
        for x in range(2):
            s0 = x0 ^ x
            parts.append(p_tile(refs, base, r, s1, s0))
            parts.append(jnp.where(s0 == 0, q_own, q_next))
        blocks.append(jnp.concatenate(parts, axis=0))
    return jnp.concatenate(blocks, axis=1)


def slot(idx, r0, s1):
    return (idx[1] ^ r0) * 2 + (idx[2] ^ s1)


def far_slot(idx, r0, s1):
    return (idx[2] ^ s1 ^ idx[4]) * 2 + (idx[1] ^ r0 ^ idx[5])


def forward_kernel(base, idx, w, *refs):
    tiles, (keep, send) = refs[:PIECES], refs[PIECES:]
    total = None
    for r0 in range(2):
        for s1 in range(2):
            term = lax.dot_general(
                w[far_slot(idx, r0, s1)], columns(idx, tiles, base, r0, s1),
                (((base,), (0,)), ((), ())), preferred_element_type=F32,
            )
            total = term if total is None else total + term
    half = total.shape[1] // 2
    low, high = total[:, :half], total[:, half:]
    keep[...] = jnp.where(idx[0] == 0, low, high)
    send[...] = jnp.where(idx[0] == 0, high, low).astype(BF)


def ordered(idx, own, other):
    mine, theirs = own[...], other[...]
    first = jnp.where(idx[0] == 0, mine, theirs)
    second = jnp.where(idx[0] == 0, theirs, mine)
    return jnp.concatenate([first, second], axis=1)


def out_grad_kernel(idx, own, other, *refs):
    tiles, out = refs[:PIECES], refs[PIECES]
    hidden = ordered(idx, own, other)
    for r0 in range(2):
        for s1 in range(2):
            out[slot(idx, r0, s1)] = lax.dot_general(
                hidden, columns(idx, tiles, 1, r0, s1), (((1,), (1,)), ((), ())),
                preferred_element_type=F32,
            ).astype(BF)


def in_grad_kernel(idx, own, other, *refs):
    tiles, out = refs[:PIECES], refs[PIECES]
    grad = ordered(idx, own, other)
    for r0 in range(2):
        for s1 in range(2):
            out[far_slot(idx, r0, s1)] = lax.dot_general(
                columns(idx, tiles, 0, r0, s1), grad, (((1,), (1,)), ((), ())),
                preferred_element_type=F32,
            ).astype(BF)


def input_grad_kernel(idx, own, other, w, *refs):
    p, q = refs[0:4], refs[4:8]
    grad = ordered(idx, own, other)
    k, n = p[0].shape[1:]
    for r0 in range(2):
        for s1 in range(2):
            block = far_slot(idx, r0, s1)
            for s0 in range(2):
                s = s1 * 2 + s0
                row = pl.multiple_of((idx[3] ^ s0) * 2 * k, 2 * k)
                term = lax.dot_general(
                    w[block, pl.ds(row, 2 * k), :], grad, (((1,), (0,)), ((), ())),
                    preferred_element_type=F32,
                ).astype(BF)
                for r1 in range(2):
                    r = r1 * 2 + r0
                    p[r][s] = term[:k, r1 * n:(r1 + 1) * n]
                    q[s][r] = term[k:, r1 * n:(r1 + 1) * n]


def near(block, axes):
    return flip(block, axes, 1), flip(block, axes, 3)


def near_and_far(block, one, three, axes):
    return (
        flip(jnp.concatenate([three[:2], block]), axes, 1),
        flip(jnp.concatenate([one[2:], block]), axes, 3),
    )


def far(one, three, axes):
    return flip(three[2:4], axes, 1), flip(one[4:], axes, 3)


def add(a, b):
    return (a.astype(F32) + b.astype(F32)).astype(BF)


def reduced_far(pieces, axes):
    own, one, two, three = pieces
    half = two.shape[0] // 2
    to_three = flip(two[:half], axes, 1)
    to_one = flip(two[half:], axes, 3)
    three = jnp.concatenate([add(three[:half], to_three), three[half:]])
    one = jnp.concatenate([one[:half], add(one[half:], to_one)])
    return own, one, three


def reduced_near(own, one, three, axes):
    first = flip(one, axes, 1).astype(F32)
    second = flip(three, axes, 3).astype(F32)
    return (own.astype(F32) + first + second).astype(BF)


def body(tokens, weight_in, weight_out, grad_out):
    t, k = tokens.shape
    f = weight_in.shape[1]
    zh = lax.axis_index("zh")
    idx = jnp.stack(
        [lax.axis_index(name) for name in ("zl1", "y0", "x1", "x0", "c", "zl0")]
    ).astype(jnp.int32)

    d = weight_in.shape[0]

    both = jnp.stack([tokens.T, grad_out.T])
    same = transposed(both, 0)
    away = transposed(both, 1)

    p, q, w1_low, w1_high = together(
        jnp.where(zh == 0, same, away), jnp.where(zh == 0, away, same),
        weight_in[: d // 2], weight_in[d // 2:],
    )
    p_next, q_next = flip(p, XAX, 1), flip(q, YAX, 1)
    w1_low = flip(w1_low, ("zl0",), 1)
    w1_high = flip(w1_high, ("zl0",), 1)

    p, q = together(jnp.stack([p, p_next]), jnp.stack([q, q_next]))
    p, q = jnp.concatenate([p, flip(p, XAX, 2)]), jnp.concatenate([q, flip(q, YAX, 2)])

    xp, xq, gp, gq, w1_low = together(p[:, 0], q[:, 0], p[:, 1], q[:, 1], w1_low)
    xp1, xp3 = near(xp, YAX)
    xq1, xq3 = near(xq, XAX)

    xp1, xp3, xq1, xq3, w1_high, w2_low, w2_high = together(
        xp1, xp3, xq1, xq3, w1_high, weight_out[: f // 2], weight_out[f // 2:]
    )
    mp1, mp3 = near_and_far(gp, xp1, xp3, YAX)
    mq1, mq3 = near_and_far(gq, xq1, xq3, XAX)
    w1_mine = jnp.stack([weight_in, jnp.concatenate([w1_low, w1_high])])
    w1 = jnp.concatenate([w1_mine, flip(w1_mine, ("c",), 1)])
    w2_low = flip(w2_low, ("zl0",), 1)
    w2_high = flip(w2_high, ("zl0",), 1)

    mp1, mp3, mq1, mq3, w2_low = together(mp1, mp3, mq1, mq3, w2_low)
    gp2 = far(mp1, mp3, YAX)
    gq2 = far(mq1, mq3, XAX)
    x_tiles = (xp, xp1, xp3, mp1, mp3, xq, xq1, xq3, mq1, mq3)
    g_tiles = (gp, mp1, mp3) + gp2 + (gq, mq1, mq3) + gq2
    w2_mine = jnp.stack([weight_out, jnp.concatenate([w2_low, w2_high])])
    w2 = jnp.concatenate([w2_mine, flip(w2_mine, ("c",), 1)])

    product = 2 * 2 * t * 4 * w1.shape[1] * f
    halves = [jax.ShapeDtypeStruct((f, t), F32), jax.ShapeDtypeStruct((f, t), BF)]
    pre_keep, pre_send = call(
        functools.partial(forward_kernel, 0), halves, idx, w1, *x_tiles, flops=product
    )
    activated, slope = gelu_parts(pre_keep + flip(pre_send, ("zl1",), 1).astype(F32))
    hidden, slope = together(activated.astype(BF), slope)
    hidden_other = flip(hidden, ("zl1",), 1)

    gh_keep, gh_send = call(
        functools.partial(forward_kernel, 1), halves, idx, w2, *g_tiles, flops=product
    )
    grad_hidden = gh_keep + flip(gh_send, ("zl1",), 1).astype(F32)
    grad_pre = (grad_hidden * slope).astype(BF)
    grad_pre_other = flip(grad_pre, ("zl1",), 1)

    (terms_out,) = call(
        out_grad_kernel, [jax.ShapeDtypeStruct(w2.shape, BF)],
        idx, hidden, hidden_other, *g_tiles, flops=product,
    )
    grad_weight_out = lax.psum_scatter(terms_out, PAIR, scatter_dimension=0)

    piece = jax.ShapeDtypeStruct((4, k, t), BF)
    pieces = call(
        input_grad_kernel, [piece] * 8, idx, grad_pre, grad_pre_other, w1, flops=product
    )
    grad_pre_late, *pieces = together(grad_pre, *pieces)
    (terms_in,) = call(
        in_grad_kernel, [jax.ShapeDtypeStruct(w1.shape, BF)],
        idx, grad_pre_late, grad_pre_other, *x_tiles, flops=product,
    )

    p_far = reduced_far(pieces[:4], YAX)
    q_far = reduced_far(pieces[4:], XAX)
    chip_terms = add(terms_in[:2], flip(terms_in[2:], ("c",), 1))
    own_terms, w1_low, w1_high = chip_terms[0], chip_terms[1, : d // 2], chip_terms[1, d // 2:]
    w1_low, p1, p3, q1, q3 = together(w1_low, *p_far[1:], *q_far[1:])
    p_sum = reduced_near(p_far[0], p1, p3, YAX)
    q_sum = reduced_near(q_far[0], q1, q3, XAX)
    w1_low = flip(w1_low, ("zl0",), 1)

    p_sum, q_sum, w1_low, w1_high = together(p_sum, q_sum, w1_low, w1_high)
    p_pair = add(p_sum[:2], flip(p_sum[2:], XAX, 2))
    q_pair = add(q_sum[:2], flip(q_sum[2:], YAX, 2))
    w1_high = flip(w1_high, ("zl0",), 1)

    p_pair, q_pair = together(p_pair, q_pair)
    p_one = add(p_pair[0], flip(p_pair[1], XAX, 1))
    q_one = add(q_pair[0], flip(q_pair[1], YAX, 1))
    p_one, q_one, w1_high = together(p_one, q_one, w1_high)
    same = transposed(jnp.where(zh == 0, p_one, q_one), 0)
    away = transposed(jnp.where(zh == 0, q_one, p_one), 1)
    grad_input = add(same, away).T
    grad_weight_in = add(own_terms, jnp.concatenate([w1_low, w1_high]))
    return grad_input, grad_weight_in, grad_weight_out


def solution(mesh):
    fine = Mesh(mesh.devices.reshape((2,) * 8), NAMES)
    in_specs = (P(GX, GY), P(GX, GY), P(GY, GX), P(GX, GY))
    out_specs = (P(GX, GY), P(GX, GY), P(GY, GX))
    return jax.shard_map(body, mesh=fine, in_specs=in_specs, out_specs=out_specs, check_vma=False)
```

```python
import functools

import jax
import jax.numpy as jnp
from jax import lax
from jax.experimental import pallas as pl
from jax.experimental.pallas import tpu as pltpu
from jax.sharding import Mesh, PartitionSpec as P

NAMES = ("zl1", "zl0", "c", "y1", "y0", "x1", "x0", "zh")
GX = ("zl1", "zl0", "c")
GY = ("y1", "y0", "x1", "x0", "zh")
YAX = ("y1", "y0")
XAX = ("x1", "x0")
BF = jnp.bfloat16
F32 = jnp.float32


def flip(value, axes, mask):
    size = 1 << len(axes)
    return lax.ppermute(value, axes, [(i, i ^ mask) for i in range(size)])


def transposed(value, flip_zh):
    pairs = []
    for a in range(2):
        for b in range(2):
            for h in range(2):
                pairs.append(((a * 2 + b) * 2 + h, (b * 2 + a) * 2 + (h ^ flip_zh)))
    return lax.ppermute(value, ("zl1", "y1", "zh"), pairs)


def together(*values):
    return lax.optimization_barrier(values)


def gelu_parts(preact):
    normal_cdf = 0.5 * (1.0 + jax.scipy.special.erf(preact * 0.7071067811865476))
    density = jnp.exp(-0.5 * preact * preact) * 0.3989422804014327
    return preact * normal_cdf, normal_cdf + preact * density


def call(kernel, outs, *operands):
    idx, *arrays = operands
    vmem = pl.BlockSpec(memory_space=pltpu.VMEM)
    return pl.pallas_call(
        kernel,
        out_shape=outs,
        in_specs=[pl.BlockSpec(memory_space=pltpu.SMEM)] + [vmem] * len(arrays),
        out_specs=[vmem] * len(outs),
        compiler_params=pltpu.CompilerParams(vmem_limit_bytes=24 * 1024 * 1024),
        cost_estimate=pl.CostEstimate(flops=1, bytes_accessed=1, transcendentals=0),
    )(idx, *arrays)


PIECES = 10


def look(refs, base, far, place):
    return [
        (0, 0), (1, 0), (3 + place // 2, -2 * (place // 2)), (2, 0),
    ][far] if base == 0 else [
        (0, 0), (1, 2), (3 + place // 2, -2 * (place // 2)), (2, 2),
    ][far]


def p_tile(refs, base, r, s1, s0):
    ref, shift = look(refs, base, r, s1 * 2)
    return refs[ref][s1 * 2 + shift + s0]


def q_tile(refs, base, r, s):
    ref, shift = look(refs, base, s, r)
    return refs[5 + ref][r + shift]


def columns(idx, refs, base, r0, s1):
    x0 = idx[2]
    blocks = []
    for r1 in range(2):
        r = r1 * 2 + r0
        parts = []
        q_own, q_next = (q_tile(refs, base, r, s1 * 2 + s0) for s0 in range(2))
        for x in range(2):
            s0 = x0 ^ x
            parts.append(p_tile(refs, base, r, s1, s0))
            parts.append(jnp.where(s0 == 0, q_own, q_next))
        blocks.append(jnp.concatenate(parts, axis=0))
    return jnp.concatenate(blocks, axis=1)


def far_slot(idx, r0, s1):
    return (idx[1] ^ s1 ^ idx[3]) * 2 + (idx[0] ^ r0 ^ idx[4])


def forward_kernel(base, idx, w, *refs):
    tiles, (keep, send) = refs[:PIECES], refs[PIECES:]
    total = None
    for r0 in range(2):
        for s1 in range(2):
            term = lax.dot_general(
                w[far_slot(idx, r0, s1)], columns(idx, tiles, base, r0, s1),
                (((base,), (0,)), ((), ())), preferred_element_type=F32,
            )
            total = term if total is None else total + term
    keep[...] = total
    send[...] = total.astype(BF)


def out_grad_kernel(idx, hidden_ref, *refs):
    tiles, out = refs[:PIECES], refs[PIECES]
    hidden = hidden_ref[...]
    for r0 in range(2):
        for s1 in range(2):
            out[far_slot(idx, r0, s1)] = lax.dot_general(
                hidden, columns(idx, tiles, 1, r0, s1), (((1,), (1,)), ((), ())),
                preferred_element_type=F32,
            ).astype(BF)


def in_grad_kernel(idx, grad_ref, *refs):
    tiles, out = refs[:PIECES], refs[PIECES]
    grad = grad_ref[...]
    for r0 in range(2):
        for s1 in range(2):
            out[far_slot(idx, r0, s1)] = lax.dot_general(
                columns(idx, tiles, 0, r0, s1), grad, (((1,), (1,)), ((), ())),
                preferred_element_type=F32,
            ).astype(BF)


def input_grad_kernel(idx, grad_ref, w, *refs):
    p, q = refs[0:4], refs[4:8]
    grad = grad_ref[...]
    k, n = p[0].shape[1:]
    for r0 in range(2):
        for s1 in range(2):
            block = far_slot(idx, r0, s1)
            for s0 in range(2):
                s = s1 * 2 + s0
                row = pl.multiple_of((idx[2] ^ s0) * 2 * k, 2 * k)
                term = lax.dot_general(
                    w[block, pl.ds(row, 2 * k), :], grad, (((1,), (0,)), ((), ())),
                    preferred_element_type=F32,
                ).astype(BF)
                for r1 in range(2):
                    r = r1 * 2 + r0
                    p[r][s] = term[:k, r1 * n:(r1 + 1) * n]
                    q[s][r] = term[k:, r1 * n:(r1 + 1) * n]


def near(block, axes):
    return flip(block, axes, 1), flip(block, axes, 3)


def near_and_far(block, one, three, axes):
    return (
        flip(jnp.concatenate([three[:2], block]), axes, 1),
        flip(jnp.concatenate([one[2:], block]), axes, 3),
    )


def far(one, three, axes):
    return flip(three[2:4], axes, 1), flip(one[4:], axes, 3)


def add(a, b):
    return (a.astype(F32) + b.astype(F32)).astype(BF)


def reduced_far(pieces, axes):
    own, one, two, three = pieces
    half = two.shape[0] // 2
    to_three = flip(two[:half], axes, 1)
    to_one = flip(two[half:], axes, 3)
    three = jnp.concatenate([add(three[:half], to_three), three[half:]])
    one = jnp.concatenate([one[:half], add(one[half:], to_one)])
    return own, one, three


def reduced_near(own, one, three, axes):
    first = flip(one, axes, 1).astype(F32)
    second = flip(three, axes, 3).astype(F32)
    return (own.astype(F32) + first + second).astype(BF)


def reduced(block, axes):
    total = block[0].astype(F32)
    for mask in (1, 3, 2):
        total = total + flip(block[mask], axes, mask).astype(F32)
    return total.astype(BF)


def body(tokens, weight_in, weight_out, grad_out):
    t, k = tokens.shape
    f = weight_in.shape[1]
    zh = lax.axis_index("zh")
    idx = jnp.stack(
        [lax.axis_index(name) for name in ("y0", "x1", "x0", "c", "zl0")]
    ).astype(jnp.int32)

    d = weight_in.shape[0]

    both = jnp.stack([tokens.T, grad_out.T])
    same = transposed(both, 0)
    away = transposed(both, 1)

    p, q, w1_low, w1_high = together(
        jnp.where(zh == 0, same, away), jnp.where(zh == 0, away, same),
        weight_in[: d // 2], weight_in[d // 2:],
    )
    p_next, q_next = flip(p, XAX, 1), flip(q, YAX, 1)
    w1_low = flip(w1_low, ("zl0",), 1)
    w1_high = flip(w1_high, ("zl0",), 1)

    p, q = together(jnp.stack([p, p_next]), jnp.stack([q, q_next]))
    p, q = jnp.concatenate([p, flip(p, XAX, 2)]), jnp.concatenate([q, flip(q, YAX, 2)])

    xp, xq, gp, gq, w1_low = together(p[:, 0], q[:, 0], p[:, 1], q[:, 1], w1_low)
    xp1, xp3 = near(xp, YAX)
    xq1, xq3 = near(xq, XAX)

    xp1, xp3, xq1, xq3, w1_high, w2_low, w2_high = together(
        xp1, xp3, xq1, xq3, w1_high, weight_out[: f // 2], weight_out[f // 2:]
    )
    mp1, mp3 = near_and_far(gp, xp1, xp3, YAX)
    mq1, mq3 = near_and_far(gq, xq1, xq3, XAX)
    w1_mine = jnp.stack([weight_in, jnp.concatenate([w1_low, w1_high])])
    w1 = jnp.concatenate([w1_mine, flip(w1_mine, ("c",), 1)])
    w2_low = flip(w2_low, ("zl0",), 1)
    w2_high = flip(w2_high, ("zl0",), 1)

    mp1, mp3, mq1, mq3, w2_low = together(mp1, mp3, mq1, mq3, w2_low)
    gp2 = far(mp1, mp3, YAX)
    gq2 = far(mq1, mq3, XAX)
    x_tiles = (xp, xp1, xp3, mp1, mp3, xq, xq1, xq3, mq1, mq3)
    g_tiles = (gp, mp1, mp3) + gp2 + (gq, mq1, mq3) + gq2
    w2_mine = jnp.stack([weight_out, jnp.concatenate([w2_low, w2_high])])
    w2 = jnp.concatenate([w2_mine, flip(w2_mine, ("c",), 1)])

    sums = [jax.ShapeDtypeStruct((f, 2 * t), F32), jax.ShapeDtypeStruct((f, 2 * t), BF)]
    pre_keep, pre_send = call(
        functools.partial(forward_kernel, 0), sums, idx, w1, *x_tiles
    )
    pre_other = flip(pre_send, ("zl1",), 1)
    gh_keep, gh_send = call(
        functools.partial(forward_kernel, 1), sums, idx, w2, *g_tiles
    )
    gh_other = flip(gh_send, ("zl1",), 1)

    pre_other, gh_keep = together(pre_other, gh_keep)
    activated, slope = gelu_parts(pre_keep + pre_other.astype(F32))
    hidden, slope = together(activated.astype(BF), slope)
    (terms_out,) = call(
        out_grad_kernel, [jax.ShapeDtypeStruct(w2.shape, BF)],
        idx, hidden, *g_tiles,
    )
    gh_other, terms_out = together(gh_other, terms_out)
    chip_out = add(terms_out[:2], flip(terms_out[2:], ("c",), 1))
    grad_pre = ((gh_keep + gh_other.astype(F32)) * slope).astype(BF)
    piece = jax.ShapeDtypeStruct((4, k, t), BF)
    pieces = call(input_grad_kernel, [piece] * 8, idx, grad_pre, w1)

    grad_pre_late, chip_out, *pieces = together(grad_pre, chip_out, *pieces)
    p_far = reduced_far(pieces[:4], YAX)
    q_far = reduced_far(pieces[4:], XAX)
    w2_low = flip(chip_out[1, : f // 2], ("zl0",), 1)
    (terms_in,) = call(
        in_grad_kernel, [jax.ShapeDtypeStruct(w1.shape, BF)], idx, grad_pre_late, *x_tiles
    )
    chip_in = add(terms_in[:2], flip(terms_in[2:], ("c",), 1))

    p1, p3, q1, q3, w2_low, w2_high, w1_low, w1_high = together(
        *p_far[1:], *q_far[1:], w2_low, chip_out[1, f // 2:],
        chip_in[1, : d // 2], chip_in[1, d // 2:],
    )
    p_sum = reduced_near(p_far[0], p1, p3, YAX)
    q_sum = reduced_near(q_far[0], q1, q3, XAX)
    w2_high = flip(w2_high, ("zl0",), 1)
    w1_low = flip(w1_low, ("zl0",), 1)

    p_sum, q_sum, w2_high, w1_high = together(p_sum, q_sum, w2_high, w1_high)
    p_one = reduced(p_sum, XAX)
    q_one = reduced(q_sum, YAX)
    w1_high = flip(w1_high, ("zl0",), 1)

    p_one, q_one, w1_low = together(p_one, q_one, w1_low)
    same = transposed(jnp.where(zh == 0, p_one, q_one), 0)
    away = transposed(jnp.where(zh == 0, q_one, p_one), 1)
    grad_input = add(same, away).T
    grad_weight_in = add(chip_in[0], jnp.concatenate([w1_low, w1_high]))
    grad_weight_out = add(chip_out[0], jnp.concatenate([w2_low, w2_high]))
    return grad_input, grad_weight_in, grad_weight_out


def solution(mesh):
    fine = Mesh(mesh.devices.reshape((2,) * 8), NAMES)
    in_specs = (P(GX, GY), P(GX, GY), P(GY, GX), P(GX, GY))
    out_specs = (P(GX, GY), P(GX, GY), P(GY, GX))
    return jax.shard_map(body, mesh=fine, in_specs=in_specs, out_specs=out_specs, check_vma=False)
```

```python
import functools

import jax
import jax.numpy as jnp
from jax import lax
from jax.experimental import pallas as pl
from jax.experimental.pallas import tpu as pltpu
from jax.sharding import Mesh, PartitionSpec as P

NAMES = ("zl1", "zl0", "c", "y1", "y0", "x1", "x0", "zh")
GX = ("zl1", "zl0", "c")
GY = ("y1", "y0", "x1", "x0", "zh")
YAX = ("y1", "y0")
XAX = ("x1", "x0")
PAIR = ("zl0", "c")
BF = jnp.bfloat16
F32 = jnp.float32


def flip(value, axes, mask):
    size = 1 << len(axes)
    return lax.ppermute(value, axes, [(i, i ^ mask) for i in range(size)])


def transposed(value, flip_zh):
    pairs = []
    for a in range(2):
        for b in range(2):
            for h in range(2):
                pairs.append(((a * 2 + b) * 2 + h, (b * 2 + a) * 2 + (h ^ flip_zh)))
    return lax.ppermute(value, ("zl1", "y1", "zh"), pairs)


def together(*values):
    return lax.optimization_barrier(values)


def gelu_parts(preact):
    normal_cdf = 0.5 * (1.0 + jax.scipy.special.erf(preact * 0.7071067811865476))
    density = jnp.exp(-0.5 * preact * preact) * 0.3989422804014327
    return preact * normal_cdf, normal_cdf + preact * density


def call(kernel, outs, *operands):
    idx, *arrays = operands
    vmem = pl.BlockSpec(memory_space=pltpu.VMEM)
    return pl.pallas_call(
        kernel,
        out_shape=outs,
        in_specs=[pl.BlockSpec(memory_space=pltpu.SMEM)] + [vmem] * len(arrays),
        out_specs=[vmem] * len(outs),
        compiler_params=pltpu.CompilerParams(vmem_limit_bytes=24 * 1024 * 1024),
        cost_estimate=pl.CostEstimate(flops=1, bytes_accessed=1, transcendentals=0),
    )(idx, *arrays)


PIECES = 8


def columns(idx, refs, r0, s1):
    x0 = idx[2]
    blocks = []
    for r1 in range(2):
        r = r1 * 2 + r0
        parts = []
        q_own, q_next = refs[4 + s1 * 2][r], refs[5 + s1 * 2][r]
        for x in range(2):
            s0 = x0 ^ x
            parts.append(refs[r][s1 * 2 + s0])
            parts.append(jnp.where(s0 == 0, q_own, q_next))
        blocks.append(jnp.concatenate(parts, axis=0))
    return jnp.concatenate(blocks, axis=1)


def slot(idx, r0, s1):
    return (idx[0] ^ r0) * 2 + (idx[1] ^ s1)


def far_slot(idx, r0, s1):
    return (idx[1] ^ s1 ^ idx[3]) * 2 + (idx[0] ^ r0 ^ idx[4])


def forward_kernel(base, idx, w, *refs):
    tiles, (keep, send) = refs[:PIECES], refs[PIECES:]
    total = None
    for r0 in range(2):
        for s1 in range(2):
            term = lax.dot_general(
                w[slot(idx, r0, s1)], columns(idx, tiles, r0, s1),
                (((base,), (0,)), ((), ())), preferred_element_type=F32,
            )
            total = term if total is None else total + term
    keep[...] = total
    send[...] = total.astype(BF)


def out_grad_kernel(idx, hidden_ref, *refs):
    tiles, out = refs[:PIECES], refs[PIECES]
    hidden = hidden_ref[...]
    for r0 in range(2):
        for s1 in range(2):
            out[far_slot(idx, r0, s1)] = lax.dot_general(
                hidden, columns(idx, tiles, r0, s1), (((1,), (1,)), ((), ())),
                preferred_element_type=F32,
            ).astype(BF)


def in_grad_kernel(idx, grad_ref, *refs):
    tiles, out = refs[:PIECES], refs[PIECES]
    grad = grad_ref[...]
    for r0 in range(2):
        for s1 in range(2):
            out[far_slot(idx, r0, s1)] = lax.dot_general(
                columns(idx, tiles, r0, s1), grad, (((1,), (1,)), ((), ())),
                preferred_element_type=F32,
            ).astype(BF)


def input_grad_kernel(idx, grad_ref, w, *refs):
    p, q = refs[0:4], refs[4:8]
    grad = grad_ref[...]
    k, n = p[0].shape[1:]
    for r0 in range(2):
        for s1 in range(2):
            block = slot(idx, r0, s1)
            for s0 in range(2):
                s = s1 * 2 + s0
                row = pl.multiple_of((idx[2] ^ s0) * 2 * k, 2 * k)
                term = lax.dot_general(
                    w[block, pl.ds(row, 2 * k), :], grad, (((1,), (0,)), ((), ())),
                    preferred_element_type=F32,
                ).astype(BF)
                for r1 in range(2):
                    r = r1 * 2 + r0
                    p[r][s] = term[:k, r1 * n:(r1 + 1) * n]
                    q[s][r] = term[k:, r1 * n:(r1 + 1) * n]


def spread(block, axes):
    two = flip(block, axes, 2)
    return [block, flip(block, axes, 1), two, flip(block, axes, 3)]


def add(a, b):
    return (a.astype(F32) + b.astype(F32)).astype(BF)


def reduced_far(pieces, axes):
    own, one, two, three = pieces
    half = two.shape[0] // 2
    to_three = flip(two[:half], axes, 1)
    to_one = flip(two[half:], axes, 3)
    three = jnp.concatenate([add(three[:half], to_three), three[half:]])
    one = jnp.concatenate([one[:half], add(one[half:], to_one)])
    return own, one, three


def reduced_near(own, one, three, axes):
    first = flip(one, axes, 1).astype(F32)
    second = flip(three, axes, 3).astype(F32)
    return (own.astype(F32) + first + second).astype(BF)


def reduced(block, axes):
    total = block[0].astype(F32)
    for mask in (1, 3, 2):
        total = total + flip(block[mask], axes, mask).astype(F32)
    return total.astype(BF)


def body(tokens, weight_in, weight_out, grad_out):
    t, k = tokens.shape
    d, f = weight_in.shape
    zh = lax.axis_index("zh")
    idx = jnp.stack(
        [lax.axis_index(name) for name in ("y0", "x1", "x0", "c", "zl0")]
    ).astype(jnp.int32)

    w1 = lax.all_gather(weight_in, PAIR, axis=0)
    w2 = lax.all_gather(weight_out, PAIR, axis=0)

    both = jnp.stack([tokens.T, grad_out.T])
    same = transposed(both, 0)
    away = transposed(both, 1)
    p, q = together(jnp.where(zh == 0, same, away), jnp.where(zh == 0, away, same))
    p, q = spread(p, XAX), spread(q, YAX)
    xp, gp, xq, gq = together(
        *(jnp.stack([tile[a] for tile in block]) for block in (p, q) for a in range(2))
    )
    xp, xq = spread(xp, YAX), spread(xq, XAX)
    gp, gq, xp[1], xq[1] = together(gp, gq, xp[1], xq[1])
    x_tiles = xp + xq

    sums = [jax.ShapeDtypeStruct((f, 2 * t), F32), jax.ShapeDtypeStruct((f, 2 * t), BF)]
    pre_keep, pre_send = call(
        functools.partial(forward_kernel, 0), sums, idx, w1, *x_tiles
    )
    pre_other = flip(pre_send, ("zl1",), 1)

    gq_two = flip(gq, XAX, 2)
    gq_late, _ = together(gq, pre_send)
    g_tiles = spread(gp, YAX) + [gq, flip(gq_late, XAX, 1), gq_two, flip(gq_late, XAX, 3)]
    gh_keep, gh_send = call(
        functools.partial(forward_kernel, 1), sums, idx, w2, *g_tiles
    )
    gh_other = flip(gh_send, ("zl1",), 1)

    pre_other, gh_keep = together(pre_other, gh_keep)
    activated, slope = gelu_parts(pre_keep + pre_other.astype(F32))
    hidden, slope = together(activated.astype(BF), slope)
    (terms_out,) = call(
        out_grad_kernel, [jax.ShapeDtypeStruct(w2.shape, BF)],
        idx, hidden, *g_tiles,
    )
    gh_other, terms_out = together(gh_other, terms_out)
    chip_out = add(terms_out[:2], flip(terms_out[2:], ("c",), 1))
    grad_pre = ((gh_keep + gh_other.astype(F32)) * slope).astype(BF)
    piece = jax.ShapeDtypeStruct((4, k, t), BF)
    pieces = call(input_grad_kernel, [piece] * 8, idx, grad_pre, w1)

    grad_pre_late, chip_out, *pieces = together(grad_pre, chip_out, *pieces)
    out_other = flip(chip_out[1], ("zl0",), 1)
    p_far = reduced_far(pieces[:4], YAX)
    q_far = reduced_far(pieces[4:], XAX)
    (terms_in,) = call(
        in_grad_kernel, [jax.ShapeDtypeStruct(w1.shape, BF)], idx, grad_pre_late, *x_tiles
    )

    chip_in = add(terms_in[:2], flip(terms_in[2:], ("c",), 1))

    p1, p3, q1, q3, chip_in = together(*p_far[1:], *q_far[1:], chip_in)
    p_sum = reduced_near(p_far[0], p1, p3, YAX)
    q_sum = reduced_near(q_far[0], q1, q3, XAX)

    p_sum, q_sum, out_other, in_low, in_high = together(
        p_sum, q_sum, out_other, chip_in[1, : d // 2], chip_in[1, d // 2:]
    )
    p_one = reduced(p_sum, XAX)
    q_one = reduced(q_sum, YAX)
    in_low = flip(in_low, ("zl0",), 1)

    p_one, q_one, in_low, in_high = together(p_one, q_one, in_low, in_high)
    in_high = flip(in_high, ("zl0",), 1)
    same = transposed(jnp.where(zh == 0, p_one, q_one), 0)
    away = transposed(jnp.where(zh == 0, q_one, p_one), 1)
    grad_input = add(same, away).T
    grad_weight_in = add(chip_in[0], jnp.concatenate([in_low, in_high]))
    grad_weight_out = add(chip_out[0], out_other)
    return grad_input, grad_weight_in, grad_weight_out


def solution(mesh):
    fine = Mesh(mesh.devices.reshape((2,) * 8), NAMES)
    in_specs = (P(GX, GY), P(GX, GY), P(GY, GX), P(GX, GY))
    out_specs = (P(GX, GY), P(GX, GY), P(GY, GX))
    return jax.shard_map(body, mesh=fine, in_specs=in_specs, out_specs=out_specs, check_vma=False)
```

```python
import functools

import jax
import jax.numpy as jnp
from jax import lax
from jax.experimental import pallas as pl
from jax.experimental.pallas import tpu as pltpu
from jax.sharding import Mesh, PartitionSpec as P

NAMES = ("zl1", "zl0", "c", "y1", "y0", "x1", "x0", "zh")
GX = ("zl1", "zl0", "c")
GY = ("y1", "y0", "x1", "x0", "zh")
YAX = ("y1", "y0")
XAX = ("x1", "x0")
BF = jnp.bfloat16
F32 = jnp.float32


def flip(value, axes, mask):
    size = 1 << len(axes)
    return lax.ppermute(value, axes, [(i, i ^ mask) for i in range(size)])


def transposed(value, flip_zh):
    pairs = []
    for a in range(2):
        for b in range(2):
            for h in range(2):
                pairs.append(((a * 2 + b) * 2 + h, (b * 2 + a) * 2 + (h ^ flip_zh)))
    return lax.ppermute(value, ("zl1", "y1", "zh"), pairs)


def together(*values):
    return lax.optimization_barrier(values)


def gelu_parts(preact):
    normal_cdf = 0.5 * (1.0 + jax.scipy.special.erf(preact * 0.7071067811865476))
    density = jnp.exp(-0.5 * preact * preact) * 0.3989422804014327
    return preact * normal_cdf, normal_cdf + preact * density


def call(kernel, outs, *operands):
    idx, *arrays = operands
    vmem = pl.BlockSpec(memory_space=pltpu.VMEM)
    return pl.pallas_call(
        kernel,
        out_shape=outs,
        in_specs=[pl.BlockSpec(memory_space=pltpu.SMEM)] + [vmem] * len(arrays),
        out_specs=[vmem] * len(outs),
        compiler_params=pltpu.CompilerParams(vmem_limit_bytes=24 * 1024 * 1024),
        cost_estimate=pl.CostEstimate(flops=1, bytes_accessed=1, transcendentals=0),
    )(idx, *arrays)


PIECES = 10


def tile_at(refs, far, place):
    if far == 2:
        return refs[3 + place // 2], place // 2 * 2
    return refs[(0, 1, None, 2)[far]], 0


def p_tile(refs, r, s1, s0):
    ref, first = tile_at(refs[:5], r, s1 * 2)
    return ref[s1 * 2 - first + s0]


def q_tile(refs, r, s):
    ref, first = tile_at(refs[5:], s, r)
    return ref[r - first]


def columns(idx, refs, r0, s1):
    x0 = idx[2]
    blocks = []
    for r1 in range(2):
        r = r1 * 2 + r0
        parts = []
        q_own, q_next = q_tile(refs, r, s1 * 2), q_tile(refs, r, s1 * 2 + 1)
        for x in range(2):
            s0 = x0 ^ x
            parts.append(p_tile(refs, r, s1, s0))
            parts.append(jnp.where(s0 == 0, q_own, q_next))
        blocks.append(jnp.concatenate(parts, axis=0))
    return jnp.concatenate(blocks, axis=1)


def far_slot(idx, r0, s1):
    return (idx[1] ^ s1 ^ idx[3]) * 2 + (idx[0] ^ r0 ^ idx[4])


def forward_kernel(base, idx, w, *refs):
    tiles, keep, sends = refs[:PIECES], refs[PIECES], refs[PIECES + 1:]
    total = None
    for r0 in range(2):
        for s1 in range(2):
            term = lax.dot_general(
                w[far_slot(idx, r0, s1)], columns(idx, tiles, r0, s1),
                (((base,), (0,)), ((), ())), preferred_element_type=F32,
            )
            total = term if total is None else total + term
    keep[...] = total
    width = total.shape[1] // len(sends)
    for i, send in enumerate(sends):
        send[...] = total[:, i * width:(i + 1) * width].astype(BF)


def out_grad_kernel(idx, hidden_ref, *refs):
    tiles, out = refs[:PIECES], refs[PIECES]
    hidden = hidden_ref[...]
    for r0 in range(2):
        for s1 in range(2):
            out[far_slot(idx, r0, s1)] = lax.dot_general(
                hidden, columns(idx, tiles, r0, s1), (((1,), (1,)), ((), ())),
                preferred_element_type=F32,
            ).astype(BF)


def in_grad_kernel(idx, grad_ref, *refs):
    tiles, out = refs[:PIECES], refs[PIECES]
    grad = grad_ref[...]
    for r0 in range(2):
        for s1 in range(2):
            out[far_slot(idx, r0, s1)] = lax.dot_general(
                columns(idx, tiles, r0, s1), grad, (((1,), (1,)), ((), ())),
                preferred_element_type=F32,
            ).astype(BF)


def input_grad_kernel(idx, grad_ref, w, *refs):
    p, q = refs[0:4], refs[4:8]
    grad = grad_ref[...]
    k, n = p[0].shape[1:]
    for r0 in range(2):
        for s1 in range(2):
            block = far_slot(idx, r0, s1)
            for s0 in range(2):
                s = s1 * 2 + s0
                row = pl.multiple_of((idx[2] ^ s0) * 2 * k, 2 * k)
                term = lax.dot_general(
                    w[block, pl.ds(row, 2 * k), :], grad, (((1,), (0,)), ((), ())),
                    preferred_element_type=F32,
                ).astype(BF)
                for r1 in range(2):
                    r = r1 * 2 + r0
                    p[r][s] = term[:k, r1 * n:(r1 + 1) * n]
                    q[s][r] = term[k:, r1 * n:(r1 + 1) * n]


def near(block, axes):
    return flip(block, axes, 1), flip(block, axes, 3)


def far(one, three, axes):
    return flip(three[:2], axes, 1), flip(one[2:], axes, 3)


def both_cores(own, arrived):
    mine = jnp.stack([own, arrived])
    return jnp.concatenate([mine, flip(mine, ("c",), 1)])


def add(a, b):
    return (a.astype(F32) + b.astype(F32)).astype(BF)


def reduced_far(pieces, axes):
    own, one, two, three = pieces
    half = two.shape[0] // 2
    to_three = flip(two[:half], axes, 1)
    to_one = flip(two[half:], axes, 3)
    three = jnp.concatenate([add(three[:half], to_three), three[half:]])
    one = jnp.concatenate([one[:half], add(one[half:], to_one)])
    return own, one, three


def reduced_near(own, one, three, axes):
    first = flip(one, axes, 1).astype(F32)
    second = flip(three, axes, 3).astype(F32)
    return (own.astype(F32) + first + second).astype(BF)


def reduced(block, axes):
    total = block[0].astype(F32)
    for mask in (1, 3, 2):
        total = total + flip(block[mask], axes, mask).astype(F32)
    return total.astype(BF)


def body(tokens, weight_in, weight_out, grad_out):
    t, k = tokens.shape
    d, f = weight_in.shape
    zh = lax.axis_index("zh")
    idx = jnp.stack(
        [lax.axis_index(name) for name in ("y0", "x1", "x0", "c", "zl0")]
    ).astype(jnp.int32)

    both = jnp.stack([tokens.T, grad_out.T])
    same, away = transposed(both, 0), transposed(both, 1)

    p, q, w1_low, w1_high = together(
        jnp.where(zh == 0, same, away), jnp.where(zh == 0, away, same),
        weight_in[: d // 2], weight_in[d // 2:],
    )
    p, q = jnp.stack([p, flip(p, XAX, 1)]), jnp.stack([q, flip(q, YAX, 1)])
    w1_low = flip(w1_low, ("zl0",), 1)

    p, q, w1_low, w1_high = together(p, q, w1_low, w1_high)
    p, q = jnp.concatenate([p, flip(p, XAX, 2)]), jnp.concatenate([q, flip(q, YAX, 2)])
    w1_high = flip(w1_high, ("zl0",), 1)

    xp, xq, gp, gq, w1_high, w2_low, w2_high = together(
        p[:, 0], q[:, 0], p[:, 1], q[:, 1], w1_high, weight_out[: f // 2], weight_out[f // 2:]
    )
    xp1, xp3 = near(xp, YAX)
    xq1, xq3 = near(xq, XAX)
    w2_low = flip(w2_low, ("zl0",), 1)

    xp1, xp3, xq1, xq3, w2_low, w2_high = together(xp1, xp3, xq1, xq3, w2_low, w2_high)
    xp2, xq2 = far(xp1, xp3, YAX), far(xq1, xq3, XAX)
    w2_high = flip(w2_high, ("zl0",), 1)
    w1 = both_cores(weight_in, jnp.concatenate([w1_low, w1_high]))

    gp, gq, w1, w2_high, *two = together(gp, gq, w1, w2_high, *xp2, *xq2)
    gp1, gp3 = near(gp, YAX)
    gq1, gq3 = near(gq, XAX)
    x_tiles = [xp, xp1, xp3] + two[:2] + [xq, xq1, xq3] + two[2:]

    kept = jax.ShapeDtypeStruct((f, 2 * t), F32)
    pre_keep, pre_first, pre_second = call(
        functools.partial(forward_kernel, 0), [kept] + [jax.ShapeDtypeStruct((f, t), BF)] * 2,
        idx, w1, *x_tiles,
    )
    pre_first = flip(pre_first, ("zl1",), 1)

    gp1, gp3, gq1, gq3, pre_first, pre_second, w2_other = together(
        gp1, gp3, gq1, gq3, pre_first, pre_second, jnp.concatenate([w2_low, w2_high])
    )
    pre_second = flip(pre_second, ("zl1",), 1)
    gp2, gq2 = far(gp1, gp3, YAX), far(gq1, gq3, XAX)
    w2 = both_cores(weight_out, w2_other)
    pre_second, w2, *two = together(pre_second, w2, *gp2, *gq2)
    pre_other = jnp.concatenate([pre_first, pre_second], axis=1)
    g_tiles = [gp, gp1, gp3] + two[:2] + [gq, gq1, gq3] + two[2:]
    activated, slope = gelu_parts(pre_keep + pre_other.astype(F32))
    hidden, slope = together(activated.astype(BF), slope)
    gh_keep, gh_send = call(
        functools.partial(forward_kernel, 1), [kept, jax.ShapeDtypeStruct((f, 2 * t), BF)],
        idx, w2, *g_tiles,
    )
    gh_other = flip(gh_send, ("zl1",), 1)

    (terms_out,) = call(
        out_grad_kernel, [jax.ShapeDtypeStruct(w2.shape, BF)],
        idx, hidden, *g_tiles,
    )
    chip_out = add(terms_out[:2], flip(terms_out[2:], ("c",), 1))
    out_low = flip(chip_out[1, : f // 2], ("zl0",), 1)
    gh_other, chip_out, out_low = together(gh_other, chip_out, out_low)
    grad_pre = ((gh_keep + gh_other.astype(F32)) * slope).astype(BF)
    piece = jax.ShapeDtypeStruct((4, k, t), BF)
    pieces = call(input_grad_kernel, [piece] * 8, idx, grad_pre, w1)

    grad_pre_late, out_high, *pieces = together(grad_pre, chip_out[1, f // 2:], *pieces)
    p_far = reduced_far(pieces[:4], YAX)
    q_far = reduced_far(pieces[4:], XAX)
    out_high = flip(out_high, ("zl0",), 1)
    (terms_in,) = call(
        in_grad_kernel, [jax.ShapeDtypeStruct(w1.shape, BF)], idx, grad_pre_late, *x_tiles
    )

    p1, p3, q1, q3, terms_in = together(*p_far[1:], *q_far[1:], terms_in)
    p_sum = reduced_near(p_far[0], p1, p3, YAX)
    q_sum = reduced_near(q_far[0], q1, q3, XAX)
    chip_in = add(terms_in[:2], flip(terms_in[2:], ("c",), 1))

    p_sum, q_sum, out_high, in_low, in_high = together(
        p_sum, q_sum, out_high, chip_in[1, : d // 2], chip_in[1, d // 2:]
    )
    p_one = reduced(p_sum, XAX)
    q_one = reduced(q_sum, YAX)
    in_low = flip(in_low, ("zl0",), 1)

    p_one, q_one, in_low, in_high = together(p_one, q_one, in_low, in_high)
    in_high = flip(in_high, ("zl0",), 1)
    same = transposed(jnp.where(zh == 0, p_one, q_one), 0)
    away = transposed(jnp.where(zh == 0, q_one, p_one), 1)
    grad_input = add(same, away).T
    grad_weight_in = add(chip_in[0], jnp.concatenate([in_low, in_high]))
    grad_weight_out = add(chip_out[0], jnp.concatenate([out_low, out_high]))
    return grad_input, grad_weight_in, grad_weight_out


def solution(mesh):
    fine = Mesh(mesh.devices.reshape((2,) * 8), NAMES)
    in_specs = (P(GX, GY), P(GX, GY), P(GY, GX), P(GX, GY))
    out_specs = (P(GX, GY), P(GX, GY), P(GY, GX))
    return jax.shard_map(body, mesh=fine, in_specs=in_specs, out_specs=out_specs, check_vma=False)
```

```python
import functools

import jax
import jax.numpy as jnp
from jax import lax
from jax.experimental import pallas as pl
from jax.experimental.pallas import tpu as pltpu
from jax.sharding import Mesh, PartitionSpec as P

NAMES = ("zl1", "zl0", "c", "y1", "y0", "x1", "x0", "zh")
GX = ("zl1", "zl0", "c")
GY = ("y1", "y0", "x1", "x0", "zh")
YAX = ("y1", "y0")
XAX = ("x1", "x0")
BF = jnp.bfloat16
F32 = jnp.float32


def flip(value, axes, mask):
    size = 1 << len(axes)
    return lax.ppermute(value, axes, [(i, i ^ mask) for i in range(size)])


def transposed(value, flip_zh):
    pairs = []
    for a in range(2):
        for b in range(2):
            for h in range(2):
                pairs.append(((a * 2 + b) * 2 + h, (b * 2 + a) * 2 + (h ^ flip_zh)))
    return lax.ppermute(value, ("zl1", "y1", "zh"), pairs)


def together(*values):
    return lax.optimization_barrier(values)


def gelu_parts(preact):
    normal_cdf = 0.5 * (1.0 + jax.scipy.special.erf(preact * 0.7071067811865476))
    density = jnp.exp(-0.5 * preact * preact) * 0.3989422804014327
    return preact * normal_cdf, normal_cdf + preact * density


def call(kernel, outs, *operands):
    idx, *arrays = operands
    vmem = pl.BlockSpec(memory_space=pltpu.VMEM)
    return pl.pallas_call(
        kernel,
        out_shape=outs,
        in_specs=[pl.BlockSpec(memory_space=pltpu.SMEM)] + [vmem] * len(arrays),
        out_specs=[vmem] * len(outs),
        compiler_params=pltpu.CompilerParams(vmem_limit_bytes=24 * 1024 * 1024),
        cost_estimate=pl.CostEstimate(flops=1, bytes_accessed=1, transcendentals=0),
    )(idx, *arrays)


PIECES = 10


def tile_at(refs, far, place):
    if far == 2:
        return refs[3 + place // 2], place // 2 * 2
    return refs[(0, 1, None, 2)[far]], 0


def p_tile(refs, r, s1, s0):
    ref, first = tile_at(refs[:5], r, s1 * 2)
    return ref[s1 * 2 - first + s0]


def q_tile(refs, r, s):
    ref, first = tile_at(refs[5:], s, r)
    return ref[r - first]


def columns(idx, refs, r0, s1):
    x0 = idx[2]
    blocks = []
    for r1 in range(2):
        r = r1 * 2 + r0
        parts = []
        q_own, q_next = q_tile(refs, r, s1 * 2), q_tile(refs, r, s1 * 2 + 1)
        for x in range(2):
            s0 = x0 ^ x
            parts.append(p_tile(refs, r, s1, s0))
            parts.append(jnp.where(s0 == 0, q_own, q_next))
        blocks.append(jnp.concatenate(parts, axis=0))
    return jnp.concatenate(blocks, axis=1)


def far_slot(idx, r0, s1):
    return (idx[1] ^ s1 ^ idx[3]) * 2 + (idx[0] ^ r0 ^ idx[4])


def forward_kernel(base, idx, w, *refs):
    tiles, keep, sends = refs[:PIECES], refs[PIECES], refs[PIECES + 1:]
    total = None
    for r0 in range(2):
        for s1 in range(2):
            term = lax.dot_general(
                w[far_slot(idx, r0, s1)], columns(idx, tiles, r0, s1),
                (((base,), (0,)), ((), ())), preferred_element_type=F32,
            )
            total = term if total is None else total + term
    keep[...] = total
    width = total.shape[1] // len(sends)
    for i, send in enumerate(sends):
        send[...] = total[:, i * width:(i + 1) * width].astype(BF)


def out_grad_kernel(idx, hidden_ref, *refs):
    tiles, out = refs[:PIECES], refs[PIECES]
    hidden = hidden_ref[...]
    for r0 in range(2):
        for s1 in range(2):
            out[far_slot(idx, r0, s1)] = lax.dot_general(
                hidden, columns(idx, tiles, r0, s1), (((1,), (1,)), ((), ())),
                preferred_element_type=F32,
            ).astype(BF)


def in_grad_kernel(idx, grad_ref, *refs):
    tiles, out = refs[:PIECES], refs[PIECES]
    grad = grad_ref[...]
    for r0 in range(2):
        for s1 in range(2):
            out[far_slot(idx, r0, s1)] = lax.dot_general(
                columns(idx, tiles, r0, s1), grad, (((1,), (1,)), ((), ())),
                preferred_element_type=F32,
            ).astype(BF)


def input_grad_kernel(idx, grad_ref, w, *refs):
    p, q = refs[0:4], refs[4:8]
    grad = grad_ref[...]
    k, n = p[0].shape[1:]
    for r0 in range(2):
        for s1 in range(2):
            block = far_slot(idx, r0, s1)
            for s0 in range(2):
                s = s1 * 2 + s0
                row = pl.multiple_of((idx[2] ^ s0) * 2 * k, 2 * k)
                term = lax.dot_general(
                    w[block, pl.ds(row, 2 * k), :], grad, (((1,), (0,)), ((), ())),
                    preferred_element_type=F32,
                ).astype(BF)
                for r1 in range(2):
                    r = r1 * 2 + r0
                    p[r][s] = term[:k, r1 * n:(r1 + 1) * n]
                    q[s][r] = term[k:, r1 * n:(r1 + 1) * n]


def near(block, axes):
    return flip(block, axes, 1), flip(block, axes, 3)


def far(one, three, axes):
    return flip(three[:2], axes, 1), flip(one[2:], axes, 3)


def both_cores(own, arrived):
    mine = jnp.stack([own, arrived])
    return jnp.concatenate([mine, flip(mine, ("c",), 1)])


def add(a, b):
    return (a.astype(F32) + b.astype(F32)).astype(BF)


def reduced_far(pieces, axes):
    own, one, two, three = pieces
    half = two.shape[0] // 2
    to_three = flip(two[:half], axes, 1)
    to_one = flip(two[half:], axes, 3)
    three = jnp.concatenate([add(three[:half], to_three), three[half:]])
    one = jnp.concatenate([one[:half], add(one[half:], to_one)])
    return own, one, three


def reduced_near(own, one, three, axes):
    first = flip(one, axes, 1).astype(F32)
    second = flip(three, axes, 3).astype(F32)
    return (own.astype(F32) + first + second).astype(BF)


def reduced(block, axes):
    total = block[0].astype(F32)
    for mask in (1, 3, 2):
        total = total + flip(block[mask], axes, mask).astype(F32)
    return total.astype(BF)


def body(tokens, weight_in, weight_out, grad_out):
    t, k = tokens.shape
    d, f = weight_in.shape
    zh = lax.axis_index("zh")
    idx = jnp.stack(
        [lax.axis_index(name) for name in ("y0", "x1", "x0", "c", "zl0")]
    ).astype(jnp.int32)

    both = jnp.stack([tokens.T, grad_out.T])
    same, away = transposed(both, 0), transposed(both, 1)

    p, q, w1_low, w1_high, idx = together(
        jnp.where(zh == 0, same, away), jnp.where(zh == 0, away, same),
        weight_in[: d // 2], weight_in[d // 2:], idx,
    )
    p, q = jnp.stack([p, flip(p, XAX, 1)]), jnp.stack([q, flip(q, YAX, 1)])
    w1_low = flip(w1_low, ("zl0",), 1)

    p, q, w1_low, w1_high, w2_low, w2_high = together(
        p, q, w1_low, w1_high, weight_out[: f // 2], weight_out[f // 2:]
    )
    p, q = jnp.concatenate([p, flip(p, XAX, 2)]), jnp.concatenate([q, flip(q, YAX, 2)])
    w1_high = flip(w1_high, ("zl0",), 1)
    w2_low = flip(w2_low, ("zl0",), 1)

    xp, xq, gp, gq, w1_high, w2_low, w2_high = together(
        p[:, 0], q[:, 0], p[:, 1], q[:, 1], w1_high, w2_low, w2_high
    )
    xp1, xp3 = near(xp, YAX)
    xq1, xq3 = near(xq, XAX)
    w2_high = flip(w2_high, ("zl0",), 1)

    xp1, xp3, xq1, xq3, w1_low, w1_high, w2_high = together(
        xp1, xp3, xq1, xq3, w1_low, w1_high, w2_high
    )
    xp2, xq2 = far(xp1, xp3, YAX), far(xq1, xq3, XAX)
    w1 = both_cores(weight_in, jnp.concatenate([w1_low, w1_high]))

    gp, gq, w1, *two = together(gp, gq, w1, *xp2, *xq2)
    gp1, gp3 = near(gp, YAX)
    gq1, gq3 = near(gq, XAX)
    x_tiles = [xp, xp1, xp3] + two[:2] + [xq, xq1, xq3] + two[2:]

    kept = jax.ShapeDtypeStruct((f, 2 * t), F32)
    pre_keep, pre_first, pre_second = call(
        functools.partial(forward_kernel, 0), [kept] + [jax.ShapeDtypeStruct((f, t), BF)] * 2,
        idx, w1, *x_tiles,
    )
    pre_first = flip(pre_first, ("zl1",), 1)

    gp1, gp3, gq1, gq3, pre_first, pre_second, w2_other = together(
        gp1, gp3, gq1, gq3, pre_first, pre_second, jnp.concatenate([w2_low, w2_high])
    )
    pre_second = flip(pre_second, ("zl1",), 1)
    gp2, gq2 = far(gp1, gp3, YAX), far(gq1, gq3, XAX)
    w2 = both_cores(weight_out, w2_other)
    pre_second, w2, *two = together(pre_second, w2, *gp2, *gq2)
    pre_other = jnp.concatenate([pre_first, pre_second], axis=1)
    g_tiles = [gp, gp1, gp3] + two[:2] + [gq, gq1, gq3] + two[2:]
    activated, slope = gelu_parts(pre_keep + pre_other.astype(F32))
    hidden, slope = together(activated.astype(BF), slope)
    gh_keep, gh_send = call(
        functools.partial(forward_kernel, 1), [kept, jax.ShapeDtypeStruct((f, 2 * t), BF)],
        idx, w2, *g_tiles,
    )
    gh_other = flip(gh_send, ("zl1",), 1)

    (terms_out,) = call(
        out_grad_kernel, [jax.ShapeDtypeStruct(w2.shape, BF)],
        idx, hidden, *g_tiles,
    )
    chip_out = add(terms_out[:2], flip(terms_out[2:], ("c",), 1))
    out_low = flip(chip_out[1, : f // 2], ("zl0",), 1)
    out_high = flip(chip_out[1, f // 2:], ("zl0",), 1)
    gh_other, chip_out, out_low, out_high = together(gh_other, chip_out, out_low, out_high)
    grad_pre = ((gh_keep + gh_other.astype(F32)) * slope).astype(BF)
    piece = jax.ShapeDtypeStruct((4, k, t), BF)
    pieces = call(input_grad_kernel, [piece] * 8, idx, grad_pre, w1)

    grad_pre_late, *pieces = together(grad_pre, *pieces)
    p_far = reduced_far(pieces[:4], YAX)
    q_far = reduced_far(pieces[4:], XAX)
    (terms_in,) = call(
        in_grad_kernel, [jax.ShapeDtypeStruct(w1.shape, BF)], idx, grad_pre_late, *x_tiles
    )

    p1, p3, q1, q3, terms_in = together(*p_far[1:], *q_far[1:], terms_in)
    p_sum = reduced_near(p_far[0], p1, p3, YAX)
    q_sum = reduced_near(q_far[0], q1, q3, XAX)
    chip_in = add(terms_in[:2], flip(terms_in[2:], ("c",), 1))
    in_low = flip(chip_in[1, : d // 2], ("zl0",), 1)

    p_sum, q_sum, in_low, in_high = together(p_sum, q_sum, in_low, chip_in[1, d // 2:])
    p_one = reduced(p_sum, XAX)
    q_one = reduced(q_sum, YAX)
    in_high = flip(in_high, ("zl0",), 1)

    p_one, q_one, in_high = together(p_one, q_one, in_high)
    same = transposed(jnp.where(zh == 0, p_one, q_one), 0)
    away = transposed(jnp.where(zh == 0, q_one, p_one), 1)
    grad_input = add(same, away).T
    grad_weight_in = add(chip_in[0], jnp.concatenate([in_low, in_high]))
    grad_weight_out = add(chip_out[0], jnp.concatenate([out_low, out_high]))
    return grad_input, grad_weight_in, grad_weight_out


def solution(mesh):
    fine = Mesh(mesh.devices.reshape((2,) * 8), NAMES)
    in_specs = (P(GX, GY), P(GX, GY), P(GY, GX), P(GX, GY))
    out_specs = (P(GX, GY), P(GX, GY), P(GY, GX))
    return jax.shard_map(body, mesh=fine, in_specs=in_specs, out_specs=out_specs, check_vma=False)
```

```python
import functools

import jax
import jax.numpy as jnp
from jax import lax
from jax.experimental import pallas as pl
from jax.experimental.pallas import tpu as pltpu
from jax.sharding import Mesh, PartitionSpec as P

NAMES = ("zl1", "zl0", "c", "y1", "y0", "x1", "x0", "zh")
GX = ("zl1", "zl0", "c")
GY = ("y1", "y0", "x1", "x0", "zh")
YAX = ("y1", "y0")
XAX = ("x1", "x0")
BF = jnp.bfloat16
F32 = jnp.float32


def flip(value, axes, mask):
    size = 1 << len(axes)
    return lax.ppermute(value, axes, [(i, i ^ mask) for i in range(size)])


def transposed(value, flip_zh):
    pairs = []
    for a in range(2):
        for b in range(2):
            for h in range(2):
                pairs.append(((a * 2 + b) * 2 + h, (b * 2 + a) * 2 + (h ^ flip_zh)))
    return lax.ppermute(value, ("zl1", "y1", "zh"), pairs)


def together(*values):
    return lax.optimization_barrier(values)


def gelu_parts(preact):
    normal_cdf = 0.5 * (1.0 + jax.scipy.special.erf(preact * 0.7071067811865476))
    density = jnp.exp(-0.5 * preact * preact) * 0.3989422804014327
    return preact * normal_cdf, normal_cdf + preact * density


def call(kernel, outs, *operands):
    idx, *arrays = operands
    vmem = pl.BlockSpec(memory_space=pltpu.VMEM)
    return pl.pallas_call(
        kernel,
        out_shape=outs,
        in_specs=[pl.BlockSpec(memory_space=pltpu.SMEM)] + [vmem] * len(arrays),
        out_specs=[vmem] * len(outs),
        compiler_params=pltpu.CompilerParams(vmem_limit_bytes=24 * 1024 * 1024),
        cost_estimate=pl.CostEstimate(flops=1, bytes_accessed=1, transcendentals=0),
    )(idx, *arrays)


PIECES = 10


def look(refs, base, far, place):
    return [
        (0, 0), (1, 0), (3 + place // 2, -2 * (place // 2)), (2, 0),
    ][far] if base == 0 else [
        (0, 0), (1, 2), (3 + place // 2, -2 * (place // 2)), (2, 2),
    ][far]


def p_tile(refs, base, r, s1, s0):
    ref, shift = look(refs, base, r, s1 * 2)
    return refs[ref][s1 * 2 + shift + s0]


def q_tile(refs, base, r, s):
    ref, shift = look(refs, base, s, r)
    return refs[5 + ref][r + shift]


def columns(idx, refs, base, mb, s1):
    x0 = idx[2]
    blocks = []
    for tb in range(2):
        r = tb * 2 + mb
        parts = []
        q_own, q_next = (q_tile(refs, base, r, s1 * 2 + s0) for s0 in range(2))
        for x in range(2):
            s0 = x0 ^ x
            parts.append(p_tile(refs, base, r, s1, s0))
            parts.append(jnp.where(s0 == 0, q_own, q_next))
        blocks.append(jnp.concatenate(parts, axis=0))
    return jnp.concatenate(blocks, axis=1)


def far_slot(idx, mb, s1):
    return (idx[1] ^ s1 ^ idx[3]) * 2 + (idx[0] ^ mb ^ idx[4])


def forward_kernel(base, idx, w, *refs):
    tiles, (keep, send) = refs[:PIECES], refs[PIECES:]
    total = None
    for mb in range(2):
        for s1 in range(2):
            term = lax.dot_general(
                w[far_slot(idx, mb, s1)], columns(idx, tiles, base, mb, s1),
                (((base,), (0,)), ((), ())), preferred_element_type=F32,
            )
            total = term if total is None else total + term
    keep[...] = total
    send[...] = total.astype(BF)


def out_grad_kernel(idx, hidden_ref, *refs):
    tiles, out = refs[:PIECES], refs[PIECES]
    hidden = hidden_ref[...]
    for mb in range(2):
        for s1 in range(2):
            out[far_slot(idx, mb, s1)] = lax.dot_general(
                hidden, columns(idx, tiles, 1, mb, s1), (((1,), (1,)), ((), ())),
                preferred_element_type=F32,
            ).astype(BF)


def in_grad_kernel(idx, grad_ref, *refs):
    tiles, out = refs[:PIECES], refs[PIECES]
    grad = grad_ref[...]
    for mb in range(2):
        for s1 in range(2):
            out[far_slot(idx, mb, s1)] = lax.dot_general(
                columns(idx, tiles, 0, mb, s1), grad, (((1,), (1,)), ((), ())),
                preferred_element_type=F32,
            ).astype(BF)


def input_grad_kernel(idx, grad_ref, w, *refs):
    p, q = refs[0:4], refs[4:8]
    grad = grad_ref[...]
    k, n = p[0].shape[1:]
    for mb in range(2):
        for s1 in range(2):
            block = far_slot(idx, mb, s1)
            for s0 in range(2):
                s = s1 * 2 + s0
                row = pl.multiple_of((idx[2] ^ s0) * 2 * k, 2 * k)
                term = lax.dot_general(
                    w[block, pl.ds(row, 2 * k), :], grad, (((1,), (0,)), ((), ())),
                    preferred_element_type=F32,
                ).astype(BF)
                for tb in range(2):
                    r = tb * 2 + mb
                    p[r][s] = term[:k, tb * n:(tb + 1) * n]
                    q[s][r] = term[k:, tb * n:(tb + 1) * n]


def near(block, axes):
    return flip(block, axes, 1), flip(block, axes, 3)


def near_and_far(block, one, three, axes):
    return (
        flip(jnp.concatenate([three[:2], block]), axes, 1),
        flip(jnp.concatenate([one[2:], block]), axes, 3),
    )


def far(one, three, axes):
    return flip(three[2:4], axes, 1), flip(one[4:], axes, 3)


def add(a, b):
    return (a.astype(F32) + b.astype(F32)).astype(BF)


def reduced_far(pieces, axes):
    own, one, two, three = pieces
    half = two.shape[0] // 2
    to_three = flip(two[:half], axes, 1)
    to_one = flip(two[half:], axes, 3)
    three = jnp.concatenate([add(three[:half], to_three), three[half:]])
    one = jnp.concatenate([one[:half], add(one[half:], to_one)])
    return own, one, three


def reduced_near(own, one, three, axes):
    first = flip(one, axes, 1).astype(F32)
    second = flip(three, axes, 3).astype(F32)
    return (own.astype(F32) + first + second).astype(BF)


def reduced(block, axes):
    total = block[0].astype(F32)
    for mask in (1, 3, 2):
        total = total + flip(block[mask], axes, mask).astype(F32)
    return total.astype(BF)


def body(tokens, weight_in, weight_out, grad_out):
    t, k = tokens.shape
    f = weight_in.shape[1]
    zh = lax.axis_index("zh")
    idx = jnp.stack(
        [lax.axis_index(name) for name in ("y0", "x1", "x0", "c", "zl0")]
    ).astype(jnp.int32)

    d = weight_in.shape[0]

    both = jnp.stack([tokens.T, grad_out.T])
    same = transposed(both, 0)
    away = transposed(both, 1)

    p, q, w1_low, w1_high, idx = together(
        jnp.where(zh == 0, same, away), jnp.where(zh == 0, away, same),
        weight_in[: d // 2], weight_in[d // 2:], idx,
    )
    p_next, q_next = flip(p, XAX, 1), flip(q, YAX, 1)
    w1_low = flip(w1_low, ("zl0",), 1)
    w1_high = flip(w1_high, ("zl0",), 1)

    p, q = together(jnp.stack([p, p_next]), jnp.stack([q, q_next]))
    p, q = jnp.concatenate([p, flip(p, XAX, 2)]), jnp.concatenate([q, flip(q, YAX, 2)])

    xp, xq, gp, gq, w1_low = together(p[:, 0], q[:, 0], p[:, 1], q[:, 1], w1_low)
    xp1, xp3 = near(xp, YAX)
    xq1, xq3 = near(xq, XAX)

    xp1, xp3, xq1, xq3, w1_high, w2_low, w2_high = together(
        xp1, xp3, xq1, xq3, w1_high, weight_out[: f // 2], weight_out[f // 2:]
    )
    mp1, mp3 = near_and_far(gp, xp1, xp3, YAX)
    mq1, mq3 = near_and_far(gq, xq1, xq3, XAX)
    w1_mine = jnp.stack([weight_in, jnp.concatenate([w1_low, w1_high])])
    w1 = jnp.concatenate([w1_mine, flip(w1_mine, ("c",), 1)])
    w2_low = flip(w2_low, ("zl0",), 1)
    w2_high = flip(w2_high, ("zl0",), 1)

    mp1, mp3, mq1, mq3, w2_low = together(mp1, mp3, mq1, mq3, w2_low)
    gp2 = far(mp1, mp3, YAX)
    gq2 = far(mq1, mq3, XAX)
    x_tiles = (xp, xp1, xp3, mp1, mp3, xq, xq1, xq3, mq1, mq3)
    w2_mine = jnp.stack([weight_out, jnp.concatenate([w2_low, w2_high])])
    w2 = jnp.concatenate([w2_mine, flip(w2_mine, ("c",), 1)])

    sums = [jax.ShapeDtypeStruct((f, 2 * t), F32), jax.ShapeDtypeStruct((f, 2 * t), BF)]
    pre_keep, pre_send = call(
        functools.partial(forward_kernel, 0), sums, idx, w1, *x_tiles
    )
    pre_other = flip(pre_send, ("zl1",), 1)
    g_tiles = (gp, mp1, mp3) + gp2 + (gq, mq1, mq3) + gq2
    gh_keep, gh_send = call(
        functools.partial(forward_kernel, 1), sums, idx, w2, *g_tiles
    )
    pre_other, gh_send = together(pre_other, gh_send)
    gh_other = flip(gh_send, ("zl1",), 1)
    activated, slope = gelu_parts(pre_keep + pre_other.astype(F32))
    hidden, slope = together(activated.astype(BF), slope)

    (terms_out,) = call(
        out_grad_kernel, [jax.ShapeDtypeStruct(w2.shape, BF)], idx, hidden, *g_tiles
    )
    chip_out = add(terms_out[:2], flip(terms_out[2:], ("c",), 1))
    out_low = flip(chip_out[1, : f // 2], ("zl0",), 1)
    gh_other, chip_out, out_low = together(gh_other, chip_out, out_low)
    grad_pre = ((gh_keep + gh_other.astype(F32)) * slope).astype(BF)
    piece = jax.ShapeDtypeStruct((4, k, t), BF)
    pieces = call(input_grad_kernel, [piece] * 8, idx, grad_pre, w1)

    grad_pre_late, *pieces = together(grad_pre, *pieces)
    p_far = reduced_far(pieces[:4], YAX)
    q_far = reduced_far(pieces[4:], XAX)
    (terms_in,) = call(
        in_grad_kernel, [jax.ShapeDtypeStruct(w1.shape, BF)], idx, grad_pre_late, *x_tiles
    )

    chip_in = add(terms_in[:2], flip(terms_in[2:], ("c",), 1))

    p1, p3, q1, q3, out_high, chip_in = together(
        *p_far[1:], *q_far[1:], chip_out[1, f // 2:], chip_in
    )
    p_sum = reduced_near(p_far[0], p1, p3, YAX)
    q_sum = reduced_near(q_far[0], q1, q3, XAX)
    out_high = flip(out_high, ("zl0",), 1)

    p_sum, q_sum, out_high, in_low, in_high = together(
        p_sum, q_sum, out_high, chip_in[1, : d // 2], chip_in[1, d // 2:]
    )
    p_one = reduced(p_sum, XAX)
    q_one = reduced(q_sum, YAX)
    in_low = flip(in_low, ("zl0",), 1)

    p_one, q_one, in_low, in_high = together(p_one, q_one, in_low, in_high)
    in_high = flip(in_high, ("zl0",), 1)
    same = transposed(jnp.where(zh == 0, p_one, q_one), 0)
    away = transposed(jnp.where(zh == 0, q_one, p_one), 1)
    grad_input = add(same, away).T
    grad_weight_in = add(chip_in[0], jnp.concatenate([in_low, in_high]))
    grad_weight_out = add(chip_out[0], jnp.concatenate([out_low, out_high]))
    return grad_input, grad_weight_in, grad_weight_out


def solution(mesh):
    fine = Mesh(mesh.devices.reshape((2,) * 8), NAMES)
    in_specs = (P(GX, GY), P(GX, GY), P(GY, GX), P(GX, GY))
    out_specs = (P(GX, GY), P(GX, GY), P(GY, GX))
    return jax.shard_map(body, mesh=fine, in_specs=in_specs, out_specs=out_specs, check_vma=False)
```

```python
import functools

import jax
import jax.numpy as jnp
from jax import lax
from jax.experimental import pallas as pl
from jax.experimental.pallas import tpu as pltpu
from jax.sharding import Mesh, PartitionSpec as P

NAMES = ("zl1", "zl0", "c", "y1", "y0", "x1", "x0", "zh")
GX = ("zl1", "zl0", "c")
GY = ("y1", "y0", "x1", "x0", "zh")
YAX = ("y1", "y0")
XAX = ("x1", "x0")
BF = jnp.bfloat16
F32 = jnp.float32


def flip(value, axes, mask):
    size = 1 << len(axes)
    return lax.ppermute(value, axes, [(i, i ^ mask) for i in range(size)])


def transposed(value, flip_zh):
    pairs = []
    for a in range(2):
        for b in range(2):
            for h in range(2):
                pairs.append(((a * 2 + b) * 2 + h, (b * 2 + a) * 2 + (h ^ flip_zh)))
    return lax.ppermute(value, ("zl1", "y1", "zh"), pairs)


def together(*values):
    return lax.optimization_barrier(values)


def gelu_parts(preact):
    normal_cdf = 0.5 * (1.0 + jax.scipy.special.erf(preact * 0.7071067811865476))
    density = jnp.exp(-0.5 * preact * preact) * 0.3989422804014327
    return preact * normal_cdf, normal_cdf + preact * density


def call(kernel, outs, *operands):
    idx, *arrays = operands
    vmem = pl.BlockSpec(memory_space=pltpu.VMEM)
    return pl.pallas_call(
        kernel,
        out_shape=outs,
        in_specs=[pl.BlockSpec(memory_space=pltpu.SMEM)] + [vmem] * len(arrays),
        out_specs=[vmem] * len(outs),
        compiler_params=pltpu.CompilerParams(vmem_limit_bytes=24 * 1024 * 1024),
        cost_estimate=pl.CostEstimate(flops=1, bytes_accessed=1, transcendentals=0),
    )(idx, *arrays)


PIECES = 10


def tile_at(refs, far, place):
    if far == 2:
        return refs[3 + place // 2], place // 2 * 2
    return refs[(0, 1, None, 2)[far]], 0


def p_tile(refs, base, r, s1, s0):
    ref, first = tile_at(refs[:5], r, s1 * 2)
    return ref[s1 * 2 - first + s0, base]


def q_tile(refs, base, r, s):
    ref, first = tile_at(refs[5:], s, r)
    return ref[r - first, base]


def columns(idx, refs, base, mb, s1):
    x0 = idx[2]
    blocks = []
    for tb in range(2):
        r = tb * 2 + mb
        parts = []
        q_own, q_next = (q_tile(refs, base, r, s1 * 2 + s0) for s0 in range(2))
        for x in range(2):
            s0 = x0 ^ x
            parts.append(p_tile(refs, base, r, s1, s0))
            parts.append(jnp.where(s0 == 0, q_own, q_next))
        blocks.append(jnp.concatenate(parts, axis=0))
    return jnp.concatenate(blocks, axis=1)


def far_slot(idx, mb, s1):
    return (idx[1] ^ s1 ^ idx[3]) * 2 + (idx[0] ^ mb ^ idx[4])


def forward_kernel(base, idx, w, *refs):
    tiles, (keep, send) = refs[:PIECES], refs[PIECES:]
    total = None
    for mb in range(2):
        for s1 in range(2):
            term = lax.dot_general(
                w[far_slot(idx, mb, s1)], columns(idx, tiles, base, mb, s1),
                (((base,), (0,)), ((), ())), preferred_element_type=F32,
            )
            total = term if total is None else total + term
    keep[...] = total
    send[...] = total.astype(BF)


def out_grad_kernel(idx, hidden_ref, *refs):
    tiles, out = refs[:PIECES], refs[PIECES]
    hidden = hidden_ref[...]
    for mb in range(2):
        for s1 in range(2):
            out[far_slot(idx, mb, s1)] = lax.dot_general(
                hidden, columns(idx, tiles, 1, mb, s1), (((1,), (1,)), ((), ())),
                preferred_element_type=F32,
            ).astype(BF)


def in_grad_kernel(idx, grad_ref, *refs):
    tiles, out = refs[:PIECES], refs[PIECES]
    grad = grad_ref[...]
    for mb in range(2):
        for s1 in range(2):
            out[far_slot(idx, mb, s1)] = lax.dot_general(
                columns(idx, tiles, 0, mb, s1), grad, (((1,), (1,)), ((), ())),
                preferred_element_type=F32,
            ).astype(BF)


def input_grad_kernel(idx, grad_ref, w, *refs):
    p, q = refs[0:4], refs[4:8]
    grad = grad_ref[...]
    k, n = p[0].shape[1:]
    for mb in range(2):
        for s1 in range(2):
            block = far_slot(idx, mb, s1)
            for s0 in range(2):
                s = s1 * 2 + s0
                row = pl.multiple_of((idx[2] ^ s0) * 2 * k, 2 * k)
                term = lax.dot_general(
                    w[block, pl.ds(row, 2 * k), :], grad, (((1,), (0,)), ((), ())),
                    preferred_element_type=F32,
                ).astype(BF)
                for tb in range(2):
                    r = tb * 2 + mb
                    p[r][s] = term[:k, tb * n:(tb + 1) * n]
                    q[s][r] = term[k:, tb * n:(tb + 1) * n]


def near(block, axes):
    return flip(block, axes, 1), flip(block, axes, 3)


def far(one, three, axes):
    return flip(three[:2], axes, 1), flip(one[2:], axes, 3)


def both_cores(own, arrived):
    mine = jnp.stack([own, arrived])
    return jnp.concatenate([mine, flip(mine, ("c",), 1)])


def add(a, b):
    return (a.astype(F32) + b.astype(F32)).astype(BF)


def reduced_far(pieces, axes):
    own, one, two, three = pieces
    half = two.shape[0] // 2
    to_three = flip(two[:half], axes, 1)
    to_one = flip(two[half:], axes, 3)
    three = jnp.concatenate([add(three[:half], to_three), three[half:]])
    one = jnp.concatenate([one[:half], add(one[half:], to_one)])
    return own, one, three


def reduced_near(own, one, three, axes):
    first = flip(one, axes, 1).astype(F32)
    second = flip(three, axes, 3).astype(F32)
    return (own.astype(F32) + first + second).astype(BF)


def reduced(block, axes):
    total = block[0].astype(F32)
    for mask in (1, 3, 2):
        total = total + flip(block[mask], axes, mask).astype(F32)
    return total.astype(BF)


def body(tokens, weight_in, weight_out, grad_out):
    t, k = tokens.shape
    f = weight_in.shape[1]
    zh = lax.axis_index("zh")
    idx = jnp.stack(
        [lax.axis_index(name) for name in ("y0", "x1", "x0", "c", "zl0")]
    ).astype(jnp.int32)

    d = weight_in.shape[0]

    both = jnp.stack([tokens.T, grad_out.T])
    same = transposed(both, 0)
    away = transposed(both, 1)

    p, q, w1_low, w1_high, idx = together(
        jnp.where(zh == 0, same, away), jnp.where(zh == 0, away, same),
        weight_in[: d // 2], weight_in[d // 2:], idx,
    )
    p_next, q_next = flip(p, XAX, 1), flip(q, YAX, 1)
    w1_low = flip(w1_low, ("zl0",), 1)
    w1_high = flip(w1_high, ("zl0",), 1)

    p, q = together(jnp.stack([p, p_next]), jnp.stack([q, q_next]))
    p, q = jnp.concatenate([p, flip(p, XAX, 2)]), jnp.concatenate([q, flip(q, YAX, 2)])

    p, q, w1_low, w2_shard = together(p, q, w1_low, weight_out)
    p1, p3 = near(p, YAX)
    q1, q3 = near(q, XAX)
    w2_other = flip(w2_shard, ("zl0",), 1)

    p1, p3, q1, q3, w1_other, w2_other = together(
        p1, p3, q1, q3, jnp.concatenate([w1_low, w1_high]), w2_other
    )
    tiles = (p, p1, p3) + far(p1, p3, YAX) + (q, q1, q3) + far(q1, q3, XAX)
    w1 = both_cores(weight_in, w1_other)
    w2 = both_cores(weight_out, w2_other)

    sums = [jax.ShapeDtypeStruct((f, 2 * t), F32), jax.ShapeDtypeStruct((f, 2 * t), BF)]
    pre_keep, pre_send = call(
        functools.partial(forward_kernel, 0), sums, idx, w1, *tiles
    )
    pre_other = flip(pre_send, ("zl1",), 1)
    gh_keep, gh_send = call(
        functools.partial(forward_kernel, 1), sums, idx, w2, *tiles
    )
    pre_other, gh_send = together(pre_other, gh_send)
    gh_other = flip(gh_send, ("zl1",), 1)
    activated, slope = gelu_parts(pre_keep + pre_other.astype(F32))
    hidden, slope = together(activated.astype(BF), slope)

    (terms_out,) = call(
        out_grad_kernel, [jax.ShapeDtypeStruct(w2.shape, BF)], idx, hidden, *tiles
    )
    chip_out = add(terms_out[:2], flip(terms_out[2:], ("c",), 1))
    out_low = flip(chip_out[1, : f // 2], ("zl0",), 1)
    gh_other, chip_out, out_low = together(gh_other, chip_out, out_low)
    grad_pre = ((gh_keep + gh_other.astype(F32)) * slope).astype(BF)
    piece = jax.ShapeDtypeStruct((4, k, t), BF)
    pieces = call(input_grad_kernel, [piece] * 8, idx, grad_pre, w1)

    grad_pre_late, *pieces = together(grad_pre, *pieces)
    p_far = reduced_far(pieces[:4], YAX)
    q_far = reduced_far(pieces[4:], XAX)
    (terms_in,) = call(
        in_grad_kernel, [jax.ShapeDtypeStruct(w1.shape, BF)], idx, grad_pre_late, *tiles
    )

    chip_in = add(terms_in[:2], flip(terms_in[2:], ("c",), 1))

    p1, p3, q1, q3, out_high, chip_in = together(
        *p_far[1:], *q_far[1:], chip_out[1, f // 2:], chip_in
    )
    p_sum = reduced_near(p_far[0], p1, p3, YAX)
    q_sum = reduced_near(q_far[0], q1, q3, XAX)
    out_high = flip(out_high, ("zl0",), 1)

    p_sum, q_sum, out_high, in_low, in_high = together(
        p_sum, q_sum, out_high, chip_in[1, : d // 2], chip_in[1, d // 2:]
    )
    p_one = reduced(p_sum, XAX)
    q_one = reduced(q_sum, YAX)
    in_low = flip(in_low, ("zl0",), 1)

    p_one, q_one, in_low, in_high = together(p_one, q_one, in_low, in_high)
    in_high = flip(in_high, ("zl0",), 1)
    same = transposed(jnp.where(zh == 0, p_one, q_one), 0)
    away = transposed(jnp.where(zh == 0, q_one, p_one), 1)
    grad_input = add(same, away).T
    grad_weight_in = add(chip_in[0], jnp.concatenate([in_low, in_high]))
    grad_weight_out = add(chip_out[0], jnp.concatenate([out_low, out_high]))
    return grad_input, grad_weight_in, grad_weight_out


def solution(mesh):
    fine = Mesh(mesh.devices.reshape((2,) * 8), NAMES)
    in_specs = (P(GX, GY), P(GX, GY), P(GY, GX), P(GX, GY))
    out_specs = (P(GX, GY), P(GX, GY), P(GY, GX))
    return jax.shard_map(body, mesh=fine, in_specs=in_specs, out_specs=out_specs, check_vma=False)
```

```python
import functools

import jax
import jax.numpy as jnp
from jax import lax
from jax.experimental import pallas as pl
from jax.experimental.pallas import tpu as pltpu
from jax.sharding import Mesh, PartitionSpec as P

NAMES = ("zl1", "zl0", "c", "y1", "y0", "x1", "x0", "zh")
GX = ("zl1", "zl0", "c")
GY = ("y1", "y0", "x1", "x0", "zh")
YAX = ("y1", "y0")
XAX = ("x1", "x0")
BF = jnp.bfloat16
F32 = jnp.float32


def flip(value, axes, mask):
    size = 1 << len(axes)
    return lax.ppermute(value, axes, [(i, i ^ mask) for i in range(size)])


def transposed(value, flip_zh):
    pairs = []
    for a in range(2):
        for b in range(2):
            for h in range(2):
                pairs.append(((a * 2 + b) * 2 + h, (b * 2 + a) * 2 + (h ^ flip_zh)))
    return lax.ppermute(value, ("zl1", "y1", "zh"), pairs)


def together(*values):
    return lax.optimization_barrier(values)


def gelu_parts(preact):
    normal_cdf = 0.5 * (1.0 + jax.scipy.special.erf(preact * 0.7071067811865476))
    density = jnp.exp(-0.5 * preact * preact) * 0.3989422804014327
    return preact * normal_cdf, normal_cdf + preact * density


def call(kernel, outs, *operands):
    idx, *arrays = operands
    vmem = pl.BlockSpec(memory_space=pltpu.VMEM)
    return pl.pallas_call(
        kernel,
        out_shape=outs,
        in_specs=[pl.BlockSpec(memory_space=pltpu.SMEM)] + [vmem] * len(arrays),
        out_specs=[vmem] * len(outs),
        compiler_params=pltpu.CompilerParams(vmem_limit_bytes=24 * 1024 * 1024),
        cost_estimate=pl.CostEstimate(flops=1, bytes_accessed=1, transcendentals=0),
    )(idx, *arrays)


PIECES = 10


def look(refs, base, far, place):
    return [
        (0, 0), (1, 0), (3 + place // 2, -2 * (place // 2)), (2, 0),
    ][far] if base == 0 else [
        (0, 0), (1, 2), (3 + place // 2, -2 * (place // 2)), (2, 2),
    ][far]


def p_tile(refs, base, r, s1, s0):
    ref, shift = look(refs, base, r, s1 * 2)
    return refs[ref][s1 * 2 + shift + s0]


def q_tile(refs, base, r, s):
    ref, shift = look(refs, base, s, r)
    return refs[5 + ref][r + shift]


def columns(idx, refs, base, mb, s1):
    x0 = idx[2]
    blocks = []
    for tb in range(2):
        r = tb * 2 + mb
        parts = []
        q_own, q_next = (q_tile(refs, base, r, s1 * 2 + s0) for s0 in range(2))
        for x in range(2):
            s0 = x0 ^ x
            parts.append(p_tile(refs, base, r, s1, s0))
            parts.append(jnp.where(s0 == 0, q_own, q_next))
        blocks.append(jnp.concatenate(parts, axis=0))
    return jnp.concatenate(blocks, axis=1)


def far_slot(idx, mb, s1):
    return (idx[1] ^ s1 ^ idx[3]) * 2 + (idx[0] ^ mb ^ idx[4])


def half_of(i, size):
    return pl.ds(pl.multiple_of(i * (size // 2), size // 2), size // 2)


def forward_kernel(base, idx, w, *refs):
    tiles, (keep, send) = refs[:PIECES], refs[PIECES:]

    @pl.loop(0, 2)
    def _(i):
        at = half_of(i, keep.shape[0])
        total = None
        for mb in range(2):
            for s1 in range(2):
                block = far_slot(idx, mb, s1)
                term = lax.dot_general(
                    w[block, :, at] if base == 0 else w[block, at, :],
                    columns(idx, tiles, base, mb, s1),
                    (((base,), (0,)), ((), ())), preferred_element_type=F32,
                )
                total = term if total is None else total + term
        keep[at, :] = total
        send[at, :] = total.astype(BF)


def out_grad_kernel(idx, hidden_ref, *refs):
    tiles, out = refs[:PIECES], refs[PIECES]

    @pl.loop(0, 2)
    def _(i):
        at = half_of(i, hidden_ref.shape[0])
        hidden = hidden_ref[at, :]
        for mb in range(2):
            for s1 in range(2):
                out[far_slot(idx, mb, s1), at, :] = lax.dot_general(
                    hidden, columns(idx, tiles, 1, mb, s1), (((1,), (1,)), ((), ())),
                    preferred_element_type=F32,
                ).astype(BF)


def in_grad_kernel(idx, grad_ref, *refs):
    tiles, out = refs[:PIECES], refs[PIECES]

    @pl.loop(0, 2)
    def _(i):
        at = half_of(i, grad_ref.shape[0])
        grad = grad_ref[at, :]
        for mb in range(2):
            for s1 in range(2):
                out[far_slot(idx, mb, s1), :, at] = lax.dot_general(
                    columns(idx, tiles, 0, mb, s1), grad, (((1,), (1,)), ((), ())),
                    preferred_element_type=F32,
                ).astype(BF)


def input_grad_kernel(idx, grad_ref, w, *refs):
    p, q = refs[0:4], refs[4:8]
    grad = grad_ref[...]
    k, n = p[0].shape[1:]
    for mb in range(2):
        for s1 in range(2):
            block = far_slot(idx, mb, s1)
            for s0 in range(2):
                s = s1 * 2 + s0
                row = pl.multiple_of((idx[2] ^ s0) * 2 * k, 2 * k)
                term = lax.dot_general(
                    w[block, pl.ds(row, 2 * k), :], grad, (((1,), (0,)), ((), ())),
                    preferred_element_type=F32,
                ).astype(BF)
                for tb in range(2):
                    r = tb * 2 + mb
                    p[r][s] = term[:k, tb * n:(tb + 1) * n]
                    q[s][r] = term[k:, tb * n:(tb + 1) * n]


def near(block, axes):
    return flip(block, axes, 1), flip(block, axes, 3)


def near_and_far(block, one, three, axes):
    return (
        flip(jnp.concatenate([three[:2], block]), axes, 1),
        flip(jnp.concatenate([one[2:], block]), axes, 3),
    )


def far(one, three, axes):
    return flip(three[2:4], axes, 1), flip(one[4:], axes, 3)


def add(a, b):
    return (a.astype(F32) + b.astype(F32)).astype(BF)


def reduced_far(pieces, axes):
    own, one, two, three = pieces
    half = two.shape[0] // 2
    to_three = flip(two[:half], axes, 1)
    to_one = flip(two[half:], axes, 3)
    three = jnp.concatenate([add(three[:half], to_three), three[half:]])
    one = jnp.concatenate([one[:half], add(one[half:], to_one)])
    return own, one, three


def reduced_near(own, one, three, axes):
    first = flip(one, axes, 1).astype(F32)
    second = flip(three, axes, 3).astype(F32)
    return (own.astype(F32) + first + second).astype(BF)


def reduced(block, axes):
    total = block[0].astype(F32)
    for mask in (1, 3, 2):
        total = total + flip(block[mask], axes, mask).astype(F32)
    return total.astype(BF)


def body(tokens, weight_in, weight_out, grad_out):
    t, k = tokens.shape
    f = weight_in.shape[1]
    zh = lax.axis_index("zh")
    idx = jnp.stack(
        [lax.axis_index(name) for name in ("y0", "x1", "x0", "c", "zl0")]
    ).astype(jnp.int32)

    d = weight_in.shape[0]

    both = jnp.stack([tokens.T, grad_out.T])
    same = transposed(both, 0)
    away = transposed(both, 1)

    p, q, w1_low, w1_high, idx = together(
        jnp.where(zh == 0, same, away), jnp.where(zh == 0, away, same),
        weight_in[: d // 2], weight_in[d // 2:], idx,
    )
    p_next, q_next = flip(p, XAX, 1), flip(q, YAX, 1)
    w1_low = flip(w1_low, ("zl0",), 1)
    w1_high = flip(w1_high, ("zl0",), 1)

    p, q = together(jnp.stack([p, p_next]), jnp.stack([q, q_next]))
    p, q = jnp.concatenate([p, flip(p, XAX, 2)]), jnp.concatenate([q, flip(q, YAX, 2)])

    xp, xq, gp, gq, w1_low = together(p[:, 0], q[:, 0], p[:, 1], q[:, 1], w1_low)
    xp1, xp3 = near(xp, YAX)
    xq1, xq3 = near(xq, XAX)

    xp1, xp3, xq1, xq3, w1_high, w2_low, w2_high = together(
        xp1, xp3, xq1, xq3, w1_high, weight_out[: f // 2], weight_out[f // 2:]
    )
    mp1, mp3 = near_and_far(gp, xp1, xp3, YAX)
    mq1, mq3 = near_and_far(gq, xq1, xq3, XAX)
    w1_mine = jnp.stack([weight_in, jnp.concatenate([w1_low, w1_high])])
    w1 = jnp.concatenate([w1_mine, flip(w1_mine, ("c",), 1)])
    w2_low = flip(w2_low, ("zl0",), 1)
    w2_high = flip(w2_high, ("zl0",), 1)

    mp1, mp3, mq1, mq3, w2_low = together(mp1, mp3, mq1, mq3, w2_low)
    gp2 = far(mp1, mp3, YAX)
    gq2 = far(mq1, mq3, XAX)
    x_tiles = (xp, xp1, xp3, mp1, mp3, xq, xq1, xq3, mq1, mq3)
    w2_mine = jnp.stack([weight_out, jnp.concatenate([w2_low, w2_high])])
    w2 = jnp.concatenate([w2_mine, flip(w2_mine, ("c",), 1)])

    sums = [jax.ShapeDtypeStruct((f, 2 * t), F32), jax.ShapeDtypeStruct((f, 2 * t), BF)]
    pre_keep, pre_send = call(
        functools.partial(forward_kernel, 0), sums, idx, w1, *x_tiles
    )
    pre_other = flip(pre_send, ("zl1",), 1)
    g_tiles = (gp, mp1, mp3) + gp2 + (gq, mq1, mq3) + gq2
    gh_keep, gh_send = call(
        functools.partial(forward_kernel, 1), sums, idx, w2, *g_tiles
    )
    pre_other, gh_send = together(pre_other, gh_send)
    gh_other = flip(gh_send, ("zl1",), 1)
    activated, slope = gelu_parts(pre_keep + pre_other.astype(F32))
    hidden, slope = together(activated.astype(BF), slope)

    (terms_out,) = call(
        out_grad_kernel, [jax.ShapeDtypeStruct(w2.shape, BF)], idx, hidden, *g_tiles
    )
    chip_out = add(terms_out[:2], flip(terms_out[2:], ("c",), 1))
    out_low = flip(chip_out[1, : f // 2], ("zl0",), 1)
    gh_other, chip_out, out_low = together(gh_other, chip_out, out_low)
    grad_pre = ((gh_keep + gh_other.astype(F32)) * slope).astype(BF)
    piece = jax.ShapeDtypeStruct((4, k, t), BF)
    pieces = call(input_grad_kernel, [piece] * 8, idx, grad_pre, w1)

    grad_pre_late, *pieces = together(grad_pre, *pieces)
    p_far = reduced_far(pieces[:4], YAX)
    q_far = reduced_far(pieces[4:], XAX)
    (terms_in,) = call(
        in_grad_kernel, [jax.ShapeDtypeStruct(w1.shape, BF)], idx, grad_pre_late, *x_tiles
    )

    chip_in = add(terms_in[:2], flip(terms_in[2:], ("c",), 1))

    p1, p3, q1, q3, out_high, chip_in = together(
        *p_far[1:], *q_far[1:], chip_out[1, f // 2:], chip_in
    )
    p_sum = reduced_near(p_far[0], p1, p3, YAX)
    q_sum = reduced_near(q_far[0], q1, q3, XAX)
    out_high = flip(out_high, ("zl0",), 1)

    p_sum, q_sum, out_high, in_low, in_high = together(
        p_sum, q_sum, out_high, chip_in[1, : d // 2], chip_in[1, d // 2:]
    )
    p_one = reduced(p_sum, XAX)
    q_one = reduced(q_sum, YAX)
    in_low = flip(in_low, ("zl0",), 1)

    p_one, q_one, in_low, in_high = together(p_one, q_one, in_low, in_high)
    in_high = flip(in_high, ("zl0",), 1)
    same = transposed(jnp.where(zh == 0, p_one, q_one), 0)
    away = transposed(jnp.where(zh == 0, q_one, p_one), 1)
    grad_input = add(same, away).T
    grad_weight_in = add(chip_in[0], jnp.concatenate([in_low, in_high]))
    grad_weight_out = add(chip_out[0], jnp.concatenate([out_low, out_high]))
    return grad_input, grad_weight_in, grad_weight_out


def solution(mesh):
    fine = Mesh(mesh.devices.reshape((2,) * 8), NAMES)
    in_specs = (P(GX, GY), P(GX, GY), P(GY, GX), P(GX, GY))
    out_specs = (P(GX, GY), P(GX, GY), P(GY, GX))
    return jax.shard_map(body, mesh=fine, in_specs=in_specs, out_specs=out_specs, check_vma=False)
```

```python
import functools

import jax
import jax.numpy as jnp
from jax import lax
from jax.experimental import pallas as pl
from jax.experimental.pallas import tpu as pltpu
from jax.sharding import Mesh, PartitionSpec as P

NAMES = ("zl1", "zl0", "c", "y1", "y0", "x1", "x0", "zh")
GX = ("zl1", "zl0", "c")
GY = ("y1", "y0", "x1", "x0", "zh")
YAX = ("y1", "y0")
XAX = ("x1", "x0")
BF = jnp.bfloat16
F32 = jnp.float32


def flip(value, axes, mask):
    size = 1 << len(axes)
    return lax.ppermute(value, axes, [(i, i ^ mask) for i in range(size)])


def transposed(value, flip_zh):
    pairs = []
    for a in range(2):
        for b in range(2):
            for h in range(2):
                pairs.append(((a * 2 + b) * 2 + h, (b * 2 + a) * 2 + (h ^ flip_zh)))
    return lax.ppermute(value, ("zl1", "y1", "zh"), pairs)


def together(*values):
    return lax.optimization_barrier(values)


def gelu_parts(preact):
    normal_cdf = 0.5 * (1.0 + jax.scipy.special.erf(preact * 0.7071067811865476))
    density = jnp.exp(-0.5 * preact * preact) * 0.3989422804014327
    return preact * normal_cdf, normal_cdf + preact * density


def call(kernel, outs, *operands):
    idx, *arrays = operands
    vmem = pl.BlockSpec(memory_space=pltpu.VMEM)
    return pl.pallas_call(
        kernel,
        out_shape=outs,
        in_specs=[pl.BlockSpec(memory_space=pltpu.SMEM)] + [vmem] * len(arrays),
        out_specs=[vmem] * len(outs),
        compiler_params=pltpu.CompilerParams(vmem_limit_bytes=24 * 1024 * 1024),
        cost_estimate=pl.CostEstimate(flops=1, bytes_accessed=1, transcendentals=0),
    )(idx, *arrays)


PIECES = 10


def look(refs, base, far, place):
    return [
        (0, 0), (1, 0), (3 + place // 2, -2 * (place // 2)), (2, 0),
    ][far] if base == 0 else [
        (0, 0), (1, 2), (3 + place // 2, -2 * (place // 2)), (2, 2),
    ][far]


def p_tile(refs, base, r, s1, s0):
    ref, shift = look(refs, base, r, s1 * 2)
    return refs[ref][s1 * 2 + shift + s0]


def q_tile(refs, base, r, s):
    ref, shift = look(refs, base, s, r)
    return refs[5 + ref][r + shift]


def columns(idx, refs, base, mb, s1):
    x0 = idx[2]
    blocks = []
    for tb in range(2):
        r = tb * 2 + mb
        parts = []
        q_own, q_next = (q_tile(refs, base, r, s1 * 2 + s0) for s0 in range(2))
        for x in range(2):
            s0 = x0 ^ x
            parts.append(p_tile(refs, base, r, s1, s0))
            parts.append(jnp.where(s0 == 0, q_own, q_next))
        blocks.append(jnp.concatenate(parts, axis=0))
    return jnp.concatenate(blocks, axis=1)


def far_slot(idx, mb, s1):
    return (idx[1] ^ s1 ^ idx[3]) * 2 + (idx[0] ^ mb ^ idx[4])


def half_of(i, size):
    return pl.ds(pl.multiple_of(i * (size // 2), size // 2), size // 2)


def forward_kernel(base, idx, w, *refs):
    tiles, (keep, send) = refs[:PIECES], refs[PIECES:]

    @pl.loop(0, 2)
    def _(i):
        at = half_of(i, keep.shape[0])
        total = None
        for mb in range(2):
            for s1 in range(2):
                block = far_slot(idx, mb, s1)
                term = lax.dot_general(
                    w[block, :, at] if base == 0 else w[block, at, :],
                    columns(idx, tiles, base, mb, s1),
                    (((base,), (0,)), ((), ())), preferred_element_type=F32,
                )
                total = term if total is None else total + term
        keep[at, :] = total
        send[at, :] = total.astype(BF)


def out_grad_kernel(idx, hidden_ref, *refs):
    tiles, out = refs[:PIECES], refs[PIECES]

    @pl.loop(0, 2)
    def _(i):
        at = half_of(i, hidden_ref.shape[0])
        hidden = hidden_ref[at, :]
        for mb in range(2):
            for s1 in range(2):
                out[far_slot(idx, mb, s1), at, :] = lax.dot_general(
                    hidden, columns(idx, tiles, 1, mb, s1), (((1,), (1,)), ((), ())),
                    preferred_element_type=F32,
                ).astype(BF)


def in_grad_kernel(idx, grad_ref, *refs):
    tiles, out = refs[:PIECES], refs[PIECES]

    @pl.loop(0, 2)
    def _(i):
        at = half_of(i, grad_ref.shape[0])
        grad = grad_ref[at, :]
        for mb in range(2):
            for s1 in range(2):
                out[far_slot(idx, mb, s1), :, at] = lax.dot_general(
                    columns(idx, tiles, 0, mb, s1), grad, (((1,), (1,)), ((), ())),
                    preferred_element_type=F32,
                ).astype(BF)


def input_grad_kernel(idx, grad_ref, w, *refs):
    p, q = refs[0:4], refs[4:8]
    grad = grad_ref[...]
    k, n = p[0].shape[1:]
    for mb in range(2):
        for s1 in range(2):
            block = far_slot(idx, mb, s1)
            for s0 in range(2):
                s = s1 * 2 + s0
                row = pl.multiple_of((idx[2] ^ s0) * 2 * k, 2 * k)
                term = lax.dot_general(
                    w[block, pl.ds(row, 2 * k), :], grad, (((1,), (0,)), ((), ())),
                    preferred_element_type=F32,
                ).astype(BF)
                for tb in range(2):
                    r = tb * 2 + mb
                    p[r][s] = term[:k, tb * n:(tb + 1) * n]
                    q[s][r] = term[k:, tb * n:(tb + 1) * n]


def near(block, axes):
    return flip(block, axes, 1), flip(block, axes, 3)


def near_and_far(block, one, three, axes):
    return (
        flip(jnp.concatenate([three[:2], block]), axes, 1),
        flip(jnp.concatenate([one[2:], block]), axes, 3),
    )


def far(one, three, axes):
    return flip(three[2:4], axes, 1), flip(one[4:], axes, 3)


def add(a, b):
    return (a.astype(F32) + b.astype(F32)).astype(BF)


def reduced_far(pieces, axes):
    own, one, two, three = pieces
    half = two.shape[0] // 2
    to_three = flip(two[:half], axes, 1)
    to_one = flip(two[half:], axes, 3)
    three = jnp.concatenate([add(three[:half], to_three), three[half:]])
    one = jnp.concatenate([one[:half], add(one[half:], to_one)])
    return own, one, three


def reduced_near(own, one, three, axes):
    first = flip(one, axes, 1).astype(F32)
    second = flip(three, axes, 3).astype(F32)
    return (own.astype(F32) + first + second).astype(BF)


def reduced(block, axes):
    total = block[0].astype(F32)
    for mask in (1, 3, 2):
        total = total + flip(block[mask], axes, mask).astype(F32)
    return total.astype(BF)


def body(tokens, weight_in, weight_out, grad_out):
    t, k = tokens.shape
    f = weight_in.shape[1]
    zh = lax.axis_index("zh")
    idx = jnp.stack(
        [lax.axis_index(name) for name in ("y0", "x1", "x0", "c", "zl0")]
    ).astype(jnp.int32)

    d = weight_in.shape[0]

    both = jnp.stack([tokens.T, grad_out.T])
    same = transposed(both, 0)
    away = transposed(both, 1)

    p, q, w1_low, w1_high, idx = together(
        jnp.where(zh == 0, same, away), jnp.where(zh == 0, away, same),
        weight_in[: d // 2], weight_in[d // 2:], idx,
    )
    p_next, q_next = flip(p, XAX, 1), flip(q, YAX, 1)
    w1_low = flip(w1_low, ("zl0",), 1)
    w1_high = flip(w1_high, ("zl0",), 1)

    p, q = together(jnp.stack([p, p_next]), jnp.stack([q, q_next]))
    p, q = jnp.concatenate([p, flip(p, XAX, 2)]), jnp.concatenate([q, flip(q, YAX, 2)])

    xp, xq, gp, gq, w1_low = together(p[:, 0], q[:, 0], p[:, 1], q[:, 1], w1_low)
    xp1, xp3 = near(xp, YAX)
    xq1, xq3 = near(xq, XAX)

    xp1, xp3, xq1, xq3, w1_high, w2_low, w2_high = together(
        xp1, xp3, xq1, xq3, w1_high, weight_out[: f // 2], weight_out[f // 2:]
    )
    mp1, mp3 = near_and_far(gp, xp1, xp3, YAX)
    mq1, mq3 = near_and_far(gq, xq1, xq3, XAX)
    w1_mine = jnp.stack([weight_in, jnp.concatenate([w1_low, w1_high])])
    w1 = jnp.concatenate([w1_mine, flip(w1_mine, ("c",), 1)])
    w2_low = flip(w2_low, ("zl0",), 1)
    w2_high = flip(w2_high, ("zl0",), 1)

    mp1, mp3, mq1, mq3, w2_low = together(mp1, mp3, mq1, mq3, w2_low)
    gp2 = far(mp1, mp3, YAX)
    gq2 = far(mq1, mq3, XAX)
    x_tiles = (xp, xp1, xp3, mp1, mp3, xq, xq1, xq3, mq1, mq3)
    w2_mine = jnp.stack([weight_out, jnp.concatenate([w2_low, w2_high])])
    w2 = jnp.concatenate([w2_mine, flip(w2_mine, ("c",), 1)])

    sums = [jax.ShapeDtypeStruct((f, 2 * t), F32), jax.ShapeDtypeStruct((f, 2 * t), BF)]
    pre_keep, pre_send = call(
        functools.partial(forward_kernel, 0), sums, idx, w1, *x_tiles
    )
    pre_other = flip(pre_send, ("zl1",), 1)
    g_tiles = (gp, mp1, mp3) + gp2 + (gq, mq1, mq3) + gq2
    gh_keep, gh_send = call(
        functools.partial(forward_kernel, 1), sums, idx, w2, *g_tiles
    )
    pre_other, gh_send = together(pre_other, gh_send)
    gh_other = flip(gh_send, ("zl1",), 1)
    activated, slope = gelu_parts(pre_keep + pre_other.astype(F32))
    hidden, slope = together(activated.astype(BF), slope)

    (terms_out,) = call(
        out_grad_kernel, [jax.ShapeDtypeStruct(w2.shape, BF)], idx, hidden, *g_tiles
    )
    chip_out = add(terms_out[:2], flip(terms_out[2:], ("c",), 1))
    out_low = flip(chip_out[1, : f // 2], ("zl0",), 1)
    gh_other, chip_out, out_low = together(gh_other, chip_out, out_low)
    grad_pre = ((gh_keep + gh_other.astype(F32)) * slope).astype(BF)
    piece = jax.ShapeDtypeStruct((4, k, t), BF)
    pieces = call(input_grad_kernel, [piece] * 8, idx, grad_pre, w1)

    p_far = reduced_far(pieces[:4], YAX)
    q_far = reduced_far(pieces[4:], XAX)

    p1, p3, q1, q3, out_high, grad_pre_late = together(
        *p_far[1:], *q_far[1:], chip_out[1, f // 2:], grad_pre
    )
    p_sum = reduced_near(p_far[0], p1, p3, YAX)
    q_sum = reduced_near(q_far[0], q1, q3, XAX)
    out_high = flip(out_high, ("zl0",), 1)
    (terms_in,) = call(
        in_grad_kernel, [jax.ShapeDtypeStruct(w1.shape, BF)], idx, grad_pre_late, *x_tiles
    )
    chip_in = add(terms_in[:2], flip(terms_in[2:], ("c",), 1))

    p_sum, q_sum, out_high, in_low, in_high = together(
        p_sum, q_sum, out_high, chip_in[1, : d // 2], chip_in[1, d // 2:]
    )
    p_one = reduced(p_sum, XAX)
    q_one = reduced(q_sum, YAX)
    in_low = flip(in_low, ("zl0",), 1)

    p_one, q_one, in_low, in_high = together(p_one, q_one, in_low, in_high)
    in_high = flip(in_high, ("zl0",), 1)
    same = transposed(jnp.where(zh == 0, p_one, q_one), 0)
    away = transposed(jnp.where(zh == 0, q_one, p_one), 1)
    grad_input = add(same, away).T
    grad_weight_in = add(chip_in[0], jnp.concatenate([in_low, in_high]))
    grad_weight_out = add(chip_out[0], jnp.concatenate([out_low, out_high]))
    return grad_input, grad_weight_in, grad_weight_out


def solution(mesh):
    fine = Mesh(mesh.devices.reshape((2,) * 8), NAMES)
    in_specs = (P(GX, GY), P(GX, GY), P(GY, GX), P(GX, GY))
    out_specs = (P(GX, GY), P(GX, GY), P(GY, GX))
    return jax.shard_map(body, mesh=fine, in_specs=in_specs, out_specs=out_specs, check_vma=False)
```
